512 devices in a mesh: row: 8 (over z_lo), col: 8 (over x, core), depth: 8 (over y, z_hi).
Axes of the slice: x: 4, y: 4, z: 16 (z_hi: 2, z_lo: 8; z = z_hi * 8 + z_lo), core: 2. Of those that a mesh axis runs over, the one named last changes fastest.
Arguments:
- query_rows: bfloat16 [8, 512, 6144], P('depth', 'col', 'row'), may hold values from -20 to 20
- key_rows: bfloat16 [8, 512, 6144], P('depth', 'col', 'row'), may hold values from -20 to 20
- value_rows: bfloat16 [8, 512, 6144], P('depth', 'col', 'row'), may hold values from -6 to 6
- positions: int32 [8, 512], P('depth'), may hold values from 0 to 511, as said below
- out_weight: bfloat16 [6144, 12288], P('row', 'col'), may hold values from -0.078125 to 0.078125
- out_grad: bfloat16 [8, 512, 12288], P('depth', 'row', 'col'), may hold values from -4 to 4
Outputs:
- layer_out: bfloat16 [8, 512, 12288], P('depth', 'row', 'col')
- query_grad: bfloat16 [8, 512, 6144], P('depth', 'col', 'row')
- key_grad: bfloat16 [8, 512, 6144], P('depth', 'col', 'row')
- value_grad: bfloat16 [8, 512, 6144], P('depth', 'col', 'row')
- weight_grad: float32 [6144, 12288], P('row', ('col', 'depth'))
The draws below stay inside these ranges and needn't reach their ends.
Inputs may be any that keep to these rules, and one draw needn't show every extreme that they name: Each row is a permutation of 0 to 511. Cut a sequence into 16 blocks of consecutive positions; tokens 512 // 8 * c to 512 // 8 * (c + 1) - 1 hold the positions of block p and of block 15 - p for some p, in some order.
All inputs are finite; a program needn't handle non-finite values.
Results may differ from the reference program's by a relative error of at most 0.035.
Values may be sent and summed in bfloat16 or wider, within the bound.
A program may use at most 128 MiB of HBM per device.

```python
import jax
import jax.numpy as jnp
from jax import lax

D = 12288
HEAD_DIM = 128
LEN = 512
SEQ_DEV = 1
HD = 6144
SEQS = 8
N_ROW = 8
N_COL = 8
N_DEPTH = 8


def position_table(key):
    base_key = jax.random.fold_in(key, 101)
    blocks = 2 * N_COL
    block_len = LEN // blocks

    def inner_order(inner_key):
        return jax.random.permutation(inner_key, block_len)

    def one_sequence(seq_key):
        pair_key, inner_key = jax.random.split(seq_key)
        first_block = jax.random.permutation(pair_key, N_COL)
        second_block = blocks - 1 - first_block
        block_ids = jnp.stack([first_block, second_block], axis=1)
        offsets = jax.vmap(inner_order)(jax.random.split(inner_key, blocks))
        offsets = offsets.reshape(N_COL, 2, block_len)
        return (block_ids[:, :, None] * block_len + offsets).reshape(LEN).astype(jnp.int32)
    return jax.vmap(one_sequence)(jax.random.split(base_key, SEQS))


def draw_positions(key, part):
    return position_table(key)


def draw_query_rows(key, part):
    key = jax.random.fold_in(key, 5)
    values = jnp.clip(jax.random.normal(key, (SEQS, LEN, HD), jnp.float32), -4.0, 4.0)
    return values.astype(jnp.bfloat16)


def draw_key_rows(key, part):
    key = jax.random.fold_in(key, 9)
    values = jnp.clip(jax.random.normal(key, (SEQS, LEN, HD), jnp.float32), -4.0, 4.0)
    return values.astype(jnp.bfloat16)


def block_scale(own_key, extent, shards, smallest, high):
    def one(dim, blocks):
        heights = jax.random.uniform(jax.random.fold_in(jax.random.fold_in(own_key, 6), dim), (blocks,), jnp.float32, smallest / len(shards), high / len(shards))
        return jnp.repeat(jnp.exp(heights), extent[dim] // blocks).reshape((-1,) + (1,) * (len(extent) - dim - 1))

    level = one(*shards[0])
    for cut in shards[1:]:
        level = level * one(*cut)
    return level


def scatter_about(stream_key, dims, width, limit, shards=(), held_as=jnp.bfloat16):
    result = jax.random.normal(stream_key, dims, jnp.float32) * width
    if len(shards) > 0:
        result = block_scale(stream_key, dims, shards, -0.22, 0.18) * result
    return jnp.clip(result, min=-limit, max=limit).astype(held_as)


def setup_inputs(seed: int = 0) -> dict:
    streams_of = jax.random.split(jax.random.key(seed), 7)
    return {
        "query_rows": draw_query_rows(jax.random.fold_in(streams_of[6], 71), 0),
        "key_rows": draw_key_rows(jax.random.fold_in(streams_of[6], 71), 0),
        "value_rows": scatter_about(streams_of[2], (SEQS, LEN, HD), 1.0, 6.0, ((0, 8), (1, 8), (2, 8))),
        "positions": draw_positions(jax.random.fold_in(streams_of[6], 71), 0),
        "out_weight": scatter_about(streams_of[4], (HD, D), HD ** -0.5, 0.078125, ((0, 8), (1, 8))),
        "out_grad": scatter_about(streams_of[5], (SEQS, LEN, D), 0.25, 4.0, ((0, 8), (1, 8), (2, 8))),
    }


def head_view(tensor):
    return tensor.reshape(tensor.shape[0], tensor.shape[1] // HEAD_DIM, HEAD_DIM).astype(jnp.float32)


def masked_logits(query_rows, key_rows, order):
    logits = jnp.einsum("qhd,khd->hqk", head_view(query_rows), head_view(key_rows)) * (HEAD_DIM ** -0.5)
    visible = order[None, None, :] <= order[None, :, None]
    return jnp.where(visible, logits, -jnp.inf)


def forward_one(inputs):
    query_rows, key_rows, value_rows, order = inputs
    logits = masked_logits(query_rows, key_rows, order)
    highest = jnp.max(logits, axis=-1)
    denominator = jnp.sum(jnp.exp(logits - highest[..., None]), axis=-1)
    probs = (jnp.exp(logits - highest[..., None]) / denominator[..., None]).astype(jnp.bfloat16)
    probs = lax.optimization_barrier(probs).astype(jnp.float32)
    context = jnp.einsum("hqk,khd->qhd", probs, head_view(value_rows))
    context = context.reshape(LEN, HD).astype(jnp.bfloat16)
    return context, highest + jnp.log(denominator)


def backward_one(inputs):
    query_rows, key_rows, value_rows, order, context, context_grad, log_norm = inputs
    head_scale = HEAD_DIM ** -0.5
    logits = masked_logits(query_rows, key_rows, order)
    weights = jnp.exp(logits - log_norm[..., None])
    row_dot = jnp.transpose(jnp.sum(head_view(context_grad) * head_view(context), axis=-1), (1, 0))
    dprob = jnp.einsum("qhd,khd->hqk", head_view(context_grad), head_view(value_rows))
    dlogits = (weights * (dprob - row_dot[..., None])).astype(jnp.bfloat16)
    dlogits = lax.optimization_barrier(dlogits).astype(jnp.float32)
    query_grad = (head_scale * jnp.einsum("hqk,khd->qhd", dlogits, head_view(key_rows))).reshape(LEN, HD)
    key_grad = (head_scale * jnp.einsum("hqk,qhd->khd", dlogits, head_view(query_rows))).reshape(LEN, HD)
    rounded_weights = lax.optimization_barrier(weights.astype(jnp.bfloat16)).astype(jnp.float32)
    value_grad = jnp.einsum("hqk,qhd->khd", rounded_weights, head_view(context_grad)).reshape(LEN, HD)
    return query_grad.astype(jnp.bfloat16), key_grad.astype(jnp.bfloat16), value_grad.astype(jnp.bfloat16)


def add_rounded(total, pair):
    first_block, second_block = pair
    product_term = jnp.einsum("slk,kn->sln", first_block.astype(jnp.float32), second_block.astype(jnp.float32))
    rounded = lax.optimization_barrier(product_term.astype(jnp.bfloat16))
    return total + rounded.astype(jnp.float32), None


def add_grad_rounded(total, pair):
    grad_block, weight_block = pair
    product_term = jnp.einsum("sln,kn->slk", grad_block.astype(jnp.float32), weight_block.astype(jnp.float32))
    rounded = lax.optimization_barrier(product_term.astype(jnp.bfloat16))
    return total + rounded.astype(jnp.float32), None


def add_group(total, pair):
    context_group, grad_group = pair
    product_term = jnp.einsum("tk,tn->kn", context_group.astype(jnp.float32), grad_group.astype(jnp.float32))
    rounded = lax.optimization_barrier(product_term.astype(jnp.bfloat16))
    return total + rounded.astype(jnp.float32), None


def reference(query_rows, key_rows, value_rows, positions, out_weight, out_grad):
    context, log_norm = lax.map(forward_one, (query_rows, key_rows, value_rows, positions))
    context_blocks = jnp.moveaxis(context.reshape(SEQS, LEN, N_ROW, HD // N_ROW), 2, 0)
    weight_rows = out_weight.reshape(N_ROW, HD // N_ROW, D)
    layer_out, unused = lax.scan(add_rounded, jnp.zeros((SEQS, LEN, D), jnp.float32), (context_blocks, weight_rows))
    grad_blocks = jnp.moveaxis(out_grad.reshape(SEQS, LEN, N_COL, D // N_COL), 2, 0)
    weight_cols = jnp.moveaxis(out_weight.reshape(HD, N_COL, D // N_COL), 1, 0)
    context_grad, unused = lax.scan(add_grad_rounded, jnp.zeros((SEQS, LEN, HD), jnp.float32), (grad_blocks, weight_cols))
    context_grad = context_grad.astype(jnp.bfloat16)
    context_groups = context.reshape(N_DEPTH, SEQ_DEV * LEN, HD)
    grad_groups = out_grad.reshape(N_DEPTH, SEQ_DEV * LEN, D)
    weight_grad, unused = lax.scan(add_group, jnp.zeros((HD, D), jnp.float32), (context_groups, grad_groups))
    query_grad, key_grad, value_grad = lax.map(backward_one, (query_rows, key_rows, value_rows, positions, context, context_grad, log_norm))
    return layer_out.astype(jnp.bfloat16), query_grad, key_grad, value_grad, weight_grad
```

```python
import functools

import jax
import jax.numpy as jnp
from jax import lax
from jax.experimental import pallas as pl
from jax.experimental.pallas import tpu as pltpu
from jax.sharding import PartitionSpec as P

HEAD_DIM = 128
HALVES = 2
SUBS = 2
MESH = pl.DeviceIdType.MESH
F32, BF16 = jnp.float32, jnp.bfloat16

NT = (((1,), (1,)), ((), ()))
TN = (((0,), (0,)), ((), ()))


def kernel(
    n_row, n_col, n_depth,
    q_ref, k_ref, v_ref, pos_ref, w_hbm, g_ref,
    out_ref, dq_ref, dk_ref, dv_ref, dw_ref,
    w_ref, qkv, pos_col, probs, probs_b, dlogits, ctx_own, ctx_all, grad_all,
    cg_stage, cg_recv, cg_own, dqkv_own, dqkv_all,
    lo, rs_stage_r, rs_stage_l, rs_r, rs_l, dw_full, dw_sum, dw_stage, dw_recv,
    w_sem, qkv_ss, qkv_rs, ag_ss, ag_rs, ctx_ss, ctx_rs, cg_ss, cg_rs, dq_ss, dq_rs,
    rs_ss, rs_rs, dw_ss, dw_rs,
):
    r, c, d = lax.axis_index("row"), lax.axis_index("col"), lax.axis_index("depth")
    y, b = lax.div(d, HALVES), lax.rem(d, HALVES)
    ring, n_y = HALVES * n_row, n_depth // HALVES
    reach = n_row // 2
    z = b * n_row + r
    span, width = q_ref.shape[1:]
    rows, cols = g_ref.shape[1:]
    length = pos_ref.shape[1]
    heads = width // HEAD_DIM
    scale = HEAD_DIM ** (-0.5)

    def on_ring(place):
        place = lax.rem(place + 2 * ring, ring)
        return {"row": lax.rem(place, n_row), "depth": y * HALVES + lax.div(place, n_row)}

    def on_y(place):
        return {"depth": lax.rem(place + n_y, n_y) * HALVES + b}

    def chunk_at(offset):
        return lax.rem(z + offset + 2 * ring, ring)

    def owner(h):
        return (h * n_col) // heads

    right, left, up, down = on_ring(z + 1), on_ring(z - 1), on_y(y + 1), on_y(y - 1)
    other = {"depth": y * HALVES + 1 - b}
    head, is_head = 0, c == owner(0)
    for h in range(1, heads):
        head = jnp.where(c >= owner(h), h, head)
        is_head = jnp.logical_or(is_head, c == owner(h))
    head_cols = pl.ds(pl.multiple_of(head * HEAD_DIM, HEAD_DIM), HEAD_DIM)
    fixed_cols = [pl.ds(h * HEAD_DIM, HEAD_DIM) for h in range(heads)]
    sub_cols = [pl.ds(u * (cols // SUBS), cols // SUBS) for u in range(SUBS)]

    def send(src, dst, send_sem, recv_sem, to):
        return pltpu.make_async_remote_copy(
            src_ref=src, dst_ref=dst, send_sem=send_sem, recv_sem=recv_sem,
            device_id=to, device_id_type=MESH,
        )

    def wait_bytes(ref, sem):
        pltpu.make_async_copy(ref, ref, sem).wait()

    barrier = pltpu.get_barrier_semaphore()
    peers = [{"col": lax.rem(c + i, n_col)} for i in range(1, n_col)]
    peers += [right, left, other, up]
    if n_y > 2:
        peers += [down]
    for peer in peers:
        pl.semaphore_signal(barrier, inc=1, device_id=peer, device_id_type=MESH)
    weight_copy = pltpu.make_async_copy(w_hbm, w_ref, w_sem)
    weight_copy.start()
    grad_all[z] = g_ref[0]
    pl.semaphore_wait(barrier, len(peers))

    drain = []

    far = [ring // 2, ring // 2 - 1]

    def grad_copy(way, step, u):
        held = chunk_at((1 - step) if way == 0 else (step - 1))
        block = grad_all.at[held, :, sub_cols[u]]
        return send(block, block, ag_ss.at[way, step - 1, u], ag_rs.at[way, step - 1, u],
                    right if way == 0 else left)

    def grad_arrives(way, step, u):
        block = grad_all.at[chunk_at(-step if way == 0 else step), :, sub_cols[u]]
        send(block, block, ag_ss.at[way, step - 1, u], ag_rs.at[way, step - 1, u], right).wait_recv()

    def grad_start(way, step, u):
        copy = grad_copy(way, step, u)
        copy.start()
        drain.append(copy.wait_send)

    def grad_step(step):
        for u in range(SUBS):
            for way in range(2):
                if step <= far[way]:
                    grad_arrives(way, step, u)
                    if step < far[way]:
                        grad_start(way, step + 1, u)

    for u in range(SUBS):
        for way in range(2):
            grad_start(way, 1, u)

    for h in range(heads):
        for t, ref in enumerate((q_ref, k_ref, v_ref)):
            place = pl.ds(pl.multiple_of(c * span, span), span)

            def copy_of(h=h, t=t, ref=ref, place=place):
                return send(ref.at[0, :, fixed_cols[h]], qkv.at[t, place, :],
                            qkv_ss.at[t, h], qkv_rs.at[t, c], {"col": owner(h)})

            @pl.when(c != owner(h))
            def _(copy_of=copy_of):
                copy_of().start()

            @pl.when(c == owner(h))
            def _(h=h, t=t, ref=ref, place=place):
                qkv[t, place, :] = ref[0, :, fixed_cols[h]]

            def wait_sent(h=h, copy_of=copy_of):
                @pl.when(c != owner(h))
                def _():
                    copy_of().wait_send()

            drain.append(wait_sent)

    block_rows = min(128, length)

    def forward(first, last):
        @pl.when(is_head)
        def _():
            @pl.loop(first, last)
            def _(i):
                at = pl.ds(pl.multiple_of(i * block_rows, block_rows), block_rows)
                logits = lax.dot_general(qkv[0, at, :], qkv[1], NT, preferred_element_type=F32)
                visible = pos_ref[...].astype(F32) <= pos_col[at, 0:1]
                logits = jnp.where(visible, logits * scale, -jnp.inf)
                highest = jnp.max(logits, axis=-1, keepdims=True)
                grown = jnp.exp(logits - highest)
                prob = grown / jnp.sum(grown, axis=-1, keepdims=True)
                probs[at, :] = prob
                rounded = prob.astype(BF16)
                probs_b[at, :] = rounded
                context = jnp.dot(rounded, qkv[2], preferred_element_type=F32)
                ctx_own[at, :] = context.astype(BF16)

    n_blocks = length // block_rows
    grad_step(1)

    @pl.when(is_head)
    def _():
        pos_col[...] = jnp.transpose(
            jnp.broadcast_to(pos_ref[...].astype(F32), (128, length))
        )
        for i in range(1, n_col):
            src = lax.rem(c + i, n_col)
            for t in range(3):
                place = qkv.at[t, pl.ds(pl.multiple_of(src * span, span), span), :]
                send(place, place, qkv_ss.at[t, 0], qkv_rs.at[t, src], {"col": src}).wait_recv()

    forward(0, n_blocks // 2)
    grad_step(2)
    forward(n_blocks // 2, n_blocks)

    def ctx_copy(half, i):
        if half == 0:
            src, place = ctx_own, b
        else:
            place = 1 - b
            src = ctx_all.at[pl.ds(pl.multiple_of(place * length, length), length), head_cols]
        dst = ctx_all.at[pl.ds(pl.multiple_of(place * length, length), length), head_cols]
        return send(src, dst, ctx_ss.at[half, i], ctx_rs.at[half, head], {"col": lax.rem(c + i, n_col)})

    def ctx_cross():
        dst = ctx_all.at[pl.ds(pl.multiple_of(b * length, length), length), head_cols]
        return send(ctx_own, dst, ctx_ss.at[0, 0], ctx_rs.at[1, head], other)

    def ctx_arrives(half, h, place_cols):
        place = b if half == 0 else 1 - b
        dst = ctx_all.at[pl.ds(pl.multiple_of(place * length, length), length), place_cols]
        send(dst, dst, ctx_ss.at[0, 0], ctx_rs.at[half, h], other).wait_recv()

    @pl.when(is_head)
    def _():
        ctx_cross().start()
        for i in range(1, n_col):
            ctx_copy(0, i).start()
        ctx_all[pl.ds(pl.multiple_of(b * length, length), length), head_cols] = ctx_own[...]

    def ctx_relay():
        @pl.when(is_head)
        def _():
            ctx_arrives(1, head, head_cols)
            for i in range(1, n_col):
                ctx_copy(1, i).start()

    def ctx_wait(half):
        for h in range(heads):
            @pl.when(c != owner(h))
            def _(h=h):
                ctx_arrives(half, h, fixed_cols[h])

    def ctx_drain():
        @pl.when(is_head)
        def _():
            ctx_cross().wait_send()
            for half in range(2):
                for i in range(1, n_col):
                    ctx_copy(half, i).wait_send()

    drain.append(ctx_drain)

    def context_grad(offset):
        block = r + offset

        @pl.when(jnp.logical_and(block >= 0, block < n_row))
        def _():
            held = chunk_at(offset)
            place = pl.ds(pl.multiple_of(block * rows, rows), rows)

            @pl.loop(0, heads // 2)
            def _(i):
                two = pl.ds(pl.multiple_of(i * 2 * HEAD_DIM, 2 * HEAD_DIM), 2 * HEAD_DIM)
                product = lax.dot_general(grad_all[held], w_ref[two, :], NT, preferred_element_type=F32)
                cg_stage[place, two] = product.astype(BF16)
                for k in range(2):
                    h = 2 * i + k
                    to = lax.div(h * n_col, heads)
                    own = pl.ds(pl.multiple_of(h * HEAD_DIM, HEAD_DIM), HEAD_DIM)

                    @pl.when(c != to)
                    def _(h=h, to=to, own=own):
                        send(cg_stage.at[place, own], cg_recv.at[c, place, :], cg_ss.at[h], cg_rs.at[c], {"col": to}).start()

                    @pl.when(c == to)
                    def _(k=k):
                        cg_recv[c, place, :] = product[:, k * HEAD_DIM:(k + 1) * HEAD_DIM].astype(BF16)

    def context_grads(first, last):
        if first == 0:
            context_grad(0)
        for step in range(max(first, 1), min(last, n_row - 1) + 1):
            @pl.loop(0, 2)
            def _(way, step=step):
                context_grad((2 * way - 1) * step)

    def cg_drain():
        for h in range(heads):
            @pl.when(c != owner(h))
            def _(h=h):
                wait_bytes(cg_recv.at[0], cg_ss.at[h])

    drain.append(cg_drain)

    tile = cols // 3

    def project(place):
        held = chunk_at(place - reach)
        tokens = ctx_all[pl.ds(pl.multiple_of(held * rows, rows), rows), :]

        @pl.loop(0, 3)
        def _(i):
            at = pl.ds(pl.multiple_of(i * tile, tile), tile)
            lo[place, :, at] = jnp.dot(tokens, w_ref[:, at], preferred_element_type=F32)

    def out_step(way, step, final=False):
        stage, landed = (rs_stage_r, rs_r) if way == 0 else (rs_stage_l, rs_l)
        place = (2 * reach - step) if way == 0 else step - 1
        for u in range(SUBS):
            total = lo[place, :, sub_cols[u]]
            if step > 1:
                block = landed.at[step - 2, :, sub_cols[u]]
                send(block, block, rs_ss.at[way, step - 2, u], rs_rs.at[way, step - 2, u], right).wait_recv()
                total = total + block[...].astype(F32)
            if final:
                lo[place, :, sub_cols[u]] = total
                continue
            stage[step - 1, :, sub_cols[u]] = total.astype(BF16)
            copy = send(stage.at[step - 1, :, sub_cols[u]], landed.at[step - 1, :, sub_cols[u]],
                        rs_ss.at[way, step - 1, u], rs_rs.at[way, step - 1, u], right if way == 0 else left)
            copy.start()
            drain.append(copy.wait_send)

    def out_both(step):
        if step < reach:
            project(2 * reach - step)
            out_step(0, step)
        if step <= reach:
            project(step - 1)
            out_step(1, step)

    stripe = cols // n_depth
    part = stripe // 2

    def weight_product(place):
        place = lax.rem(place + 2 * n_y, n_y)
        at = pl.ds(pl.multiple_of(place * 2 * stripe + b * 128, 128), 256)
        tokens = grad_all[:, :, at].reshape(ring * rows, 256)
        dw_full[...] = lax.dot_general(tokens, ctx_all[...], TN, preferred_element_type=F32)
        dw_sum[place] = dw_full[pl.ds(pl.multiple_of(b * 64, 64), stripe), :]

    def weight_step(way, step, final=False):
        place = lax.rem(y + (-step if way == 0 else step) + 2 * n_y, n_y)
        own = slice(way * part, (way + 1) * part)
        total = dw_sum[place, own, :]
        if step > 1:
            block = dw_recv.at[way, step - 2]
            send(block, block, dw_ss.at[way, step - 2], dw_rs.at[way, step - 2], up).wait_recv()
            total = total + block[...].astype(F32)
        if final:
            dw_ref[own, :] = total
            return
        dw_stage[way, step - 1] = total.astype(BF16)
        copy = send(dw_stage.at[way, step - 1], dw_recv.at[way, step - 1], dw_ss.at[way, step - 1],
                    dw_rs.at[way, step - 1], up if way == 0 else down)
        copy.start()
        drain.append(copy.wait_send)

    def backward():
        @pl.when(is_head)
        def _():
            for i in range(1, n_col):
                src = lax.rem(c + i, n_col)
                wait_bytes(cg_recv.at[src], cg_rs.at[src])

            @pl.loop(0, n_blocks)
            def _(i):
                at = pl.ds(pl.multiple_of(i * block_rows, block_rows), block_rows)
                total = cg_recv[0, at, :].astype(F32)
                for k in range(1, n_col):
                    total = total + cg_recv[k, at, :].astype(F32)
                grad = total.astype(BF16)
                cg_own[at, :] = grad
                row_dot = jnp.sum(grad.astype(F32) * ctx_own[at, :].astype(F32), axis=-1, keepdims=True)
                dprob = lax.dot_general(grad, qkv[2], NT, preferred_element_type=F32)
                rounded = (probs[at, :] * (dprob - row_dot)).astype(BF16)
                dlogits[at, :] = rounded
                query_grad = jnp.dot(rounded, qkv[1], preferred_element_type=F32) * scale
                dqkv_own[0, at, :] = query_grad.astype(BF16)

            key_grad = lax.dot_general(dlogits[...], qkv[0], TN, preferred_element_type=F32) * scale
            dqkv_own[1] = key_grad.astype(BF16)
            value_grad = lax.dot_general(probs_b[...], cg_own[...], TN, preferred_element_type=F32)
            dqkv_own[2] = value_grad.astype(BF16)
            for t in range(3):
                for i in range(1, n_col):
                    dqkv_copy(t, i).start()
                dqkv_all[t, :, head_cols] = dqkv_own[t, pl.ds(pl.multiple_of(c * span, span), span), :]

    def dqkv_copy(t, i):
        to = lax.rem(c + i, n_col)
        return send(dqkv_own.at[t, pl.ds(pl.multiple_of(to * span, span), span), :],
                    dqkv_all.at[t, :, head_cols], dq_ss.at[t, i], dq_rs.at[t, head], {"col": to})

    def dqkv_drain():
        @pl.when(is_head)
        def _():
            for t in range(3):
                for i in range(1, n_col):
                    dqkv_copy(t, i).wait_send()

    drain.append(dqkv_drain)

    last = ring // 2
    weight_copy.wait()
    context_grads(0, 1)
    grad_step(3) if last >= 3 else None
    context_grads(2, 3)
    grad_step(4) if last >= 4 else None
    ctx_relay()
    context_grads(4, 4)
    grad_step(5) if last >= 5 else None
    ctx_wait(0)
    ctx_wait(1)
    out_both(1)
    grad_step(6) if last >= 6 else None
    context_grads(5, 6)
    out_both(2)
    grad_step(7) if last >= 7 else None
    context_grads(7, n_row)
    out_both(3)
    for step in range(8, last + 1):
        grad_step(step)
    for step in range(4, reach + 1):
        out_both(step)
    project(reach)
    for offset in (-1, 1):
        weight_product(y + offset)
        weight_step(0 if offset < 0 else 1, 1)
    for offset in range(2, n_y - 1):
        weight_product(y + offset)
    weight_product(y)
    backward()
    for step in range(2, n_y):
        weight_step(0, step)
        weight_step(1, step)
    out_step(0, reach, final=True)
    out_step(1, reach + 1, final=True)
    out_ref[0] = lo[reach].astype(BF16)
    weight_step(0, n_y, final=True)
    weight_step(1, n_y, final=True)
    for t, ref in enumerate((dq_ref, dk_ref, dv_ref)):
        for h in range(heads):
            @pl.when(c != owner(h))
            def _(t=t, h=h):
                block = dqkv_all.at[t, :, fixed_cols[h]]
                send(block, block, dq_ss.at[t, 0], dq_rs.at[t, h], other).wait_recv()
        ref[0] = dqkv_all[t]
    for wait in drain:
        wait()


def solution(mesh):
    n_row, n_col, n_depth = mesh.shape["row"], mesh.shape["col"], mesh.shape["depth"]

    def local(q, k, v, positions, weight, grad):
        _, span, width = q.shape
        _, rows, cols = grad.shape
        length = positions.shape[1]
        heads, ring, reach, n_y = width // HEAD_DIM, HALVES * n_row, n_row // 2, n_depth // HALVES
        stripe = cols // n_depth
        vmem = pl.BlockSpec(memory_space=pltpu.VMEM)
        dma = pltpu.SemaphoreType.DMA
        hops, turns = max(reach, 1), max(n_y - 1, 1)
        scratch = [
            pltpu.VMEM((width, cols), BF16),
            pltpu.VMEM((3, length, HEAD_DIM), BF16),
            pltpu.VMEM((length, 128), F32),
            pltpu.VMEM((length, length), F32),
            pltpu.VMEM((length, length), BF16),
            pltpu.VMEM((length, length), BF16),
            pltpu.VMEM((length, HEAD_DIM), BF16),
            pltpu.VMEM((HALVES * length, width), BF16),
            pltpu.VMEM((ring, rows, cols), BF16),
            pltpu.VMEM((length, width), BF16),
            pltpu.VMEM((n_col, length, HEAD_DIM), BF16),
            pltpu.VMEM((length, HEAD_DIM), BF16),
            pltpu.VMEM((3, length, HEAD_DIM), BF16),
            pltpu.VMEM((3, span, width), BF16),
            pltpu.VMEM((2 * reach, rows, cols), F32),
            pltpu.VMEM((hops, rows, cols), BF16),
            pltpu.VMEM((hops, rows, cols), BF16),
            pltpu.VMEM((hops, rows, cols), BF16),
            pltpu.VMEM((hops, rows, cols), BF16),
            pltpu.VMEM((256, width), F32),
            pltpu.VMEM((n_y, stripe, width), F32),
            pltpu.VMEM((2, turns, stripe // 2, width), BF16),
            pltpu.VMEM((2, turns, stripe // 2, width), BF16),
            dma,
            dma((3, heads)), dma((3, n_col)),
            dma((2, ring // 2, SUBS)), dma((2, ring // 2, SUBS)),
            dma((2, n_col)), dma((2, heads)),
            dma((heads,)), dma((n_col,)),
            dma((3, n_col)), dma((3, heads)),
            dma((2, hops, SUBS)), dma((2, hops, SUBS)),
            dma((2, turns)), dma((2, turns)),
        ]
        layer_out, query_grad, key_grad, value_grad, weight_grad = pl.pallas_call(
            functools.partial(kernel, n_row, n_col, n_depth),
            out_shape=(
                jax.ShapeDtypeStruct(grad.shape, BF16),
                jax.ShapeDtypeStruct(q.shape, BF16),
                jax.ShapeDtypeStruct(k.shape, BF16),
                jax.ShapeDtypeStruct(v.shape, BF16),
                jax.ShapeDtypeStruct((stripe, width), F32),
            ),
            in_specs=[vmem] * 4 + [pl.BlockSpec(memory_space=pl.ANY), vmem],
            out_specs=(vmem,) * 5,
            scratch_shapes=scratch,
            compiler_params=pltpu.CompilerParams(
                collective_id=0, has_side_effects=True, vmem_limit_bytes=56 * 1024 * 1024
            ),
        )(q, k, v, positions, weight, grad)
        return layer_out, query_grad, key_grad, value_grad, weight_grad.T

    return jax.shard_map(
        local,
        mesh=mesh,
        in_specs=(
            P("depth", "col", "row"),
            P("depth", "col", "row"),
            P("depth", "col", "row"),
            P("depth", None),
            P("row", "col"),
            P("depth", "row", "col"),
        ),
        out_specs=(
            P("depth", "row", "col"),
            P("depth", "col", "row"),
            P("depth", "col", "row"),
            P("depth", "col", "row"),
            P("row", ("col", "depth")),
        ),
        check_vma=False,
    )
```

```python
import functools

import jax
import jax.numpy as jnp
from jax import lax
from jax.experimental import pallas as pl
from jax.experimental.pallas import tpu as pltpu
from jax.sharding import PartitionSpec as P

HEAD_DIM = 128
HALVES = 2
SUBS = 2
VMEM_BYTES = 56 * 1024 * 1024
MESH = pl.DeviceIdType.MESH
F32, BF16 = jnp.float32, jnp.bfloat16

NT = (((1,), (1,)), ((), ()))
TN = (((0,), (0,)), ((), ()))


def kernel(
    n_row, n_col, n_depth,
    q_ref, k_ref, v_ref, pos_ref, w_hbm, g_ref,
    out_ref, dq_ref, dk_ref, dv_ref, dw_ref,
    w_ref, qkv, pos_col, probs, probs_b, dlogits, ctx_own, ctx_all, ctx_rel, relay, grad_all,
    cg_stage, cg_recv, cg_own, dqkv_own, dqkv_all,
    lo, rs_stage_r, rs_stage_l, rs_r, rs_l, dw_sum, dw_stage, dw_recv,
    w_sem, qkv_ss, qkv_rs, ag_ss, ag_rs, ctx_ss, ctx_rs, fwd_ss, cross_ss, cross_rs, cg_ss, cg_rs, dq_ss, dq_rs,
    rs_ss, rs_rs, dw_ss, dw_rs,
):
    r, c, d = lax.axis_index("row"), lax.axis_index("col"), lax.axis_index("depth")
    y, b = lax.div(d, HALVES), lax.rem(d, HALVES)
    ring, n_y = HALVES * n_row, n_depth // HALVES
    reach = n_row // 2
    z = b * n_row + r
    span, width = q_ref.shape[1:]
    rows, cols = g_ref.shape[1:]
    length = pos_ref.shape[1]
    heads = width // HEAD_DIM
    scale = HEAD_DIM ** (-0.5)

    def on_ring(place):
        place = lax.rem(place + 2 * ring, ring)
        return {"row": lax.rem(place, n_row), "depth": y * HALVES + lax.div(place, n_row)}

    def on_y(place):
        return {"depth": lax.rem(place + n_y, n_y) * HALVES + b}

    def chunk_at(offset):
        return lax.rem(z + turn * offset + 2 * ring, ring)

    def owner(h):
        return (h * n_col) // heads

    core = lax.rem(c, 2)
    turn = 1 - 2 * core
    right, left, up, down = on_ring(z + turn), on_ring(z - turn), on_y(y + 1), on_y(y - 1)
    sibling = {"col": c + 1 - 2 * core}
    far_right, far_left = on_ring(z + turn * (n_row - 1)), on_ring(z - turn * (n_row - 1))
    middle = ring // 2
    head, is_head = 0, c == owner(0)
    for h in range(1, heads):
        head = jnp.where(c >= owner(h), h, head)
        is_head = jnp.logical_or(is_head, c == owner(h))
    head_cols = pl.ds(pl.multiple_of(head * HEAD_DIM, HEAD_DIM), HEAD_DIM)
    fixed_cols = [pl.ds(h * HEAD_DIM, HEAD_DIM) for h in range(heads)]
    sub_cols = [pl.ds(u * (cols // SUBS), cols // SUBS) for u in range(SUBS)]

    def send(src, dst, send_sem, recv_sem, to):
        return pltpu.make_async_remote_copy(
            src_ref=src, dst_ref=dst, send_sem=send_sem, recv_sem=recv_sem,
            device_id=to, device_id_type=MESH,
        )

    def wait_bytes(ref, sem):
        pltpu.make_async_copy(ref, ref, sem).wait()

    barrier = pltpu.get_barrier_semaphore()
    peers = [{"col": lax.rem(c + i, n_col)} for i in range(1, n_col)]
    peers += [right, left, up]
    if n_y > 2:
        peers += [down]
    if n_row > 2:
        peers += [far_right, far_left]
    for peer in peers:
        pl.semaphore_signal(barrier, inc=1, device_id=peer, device_id_type=MESH)
    weight_copy = pltpu.make_async_copy(w_hbm, w_ref, w_sem)
    weight_copy.start()
    grad_all[middle] = g_ref[0]
    pl.semaphore_wait(barrier, len(peers))

    drain = []

    far = [ring // 2, ring // 2 - 1]

    def grad_copy(way, step, u):
        sign = -1 if way == 0 else 1
        return send(grad_all.at[middle + sign * (step - 1), :, sub_cols[u]],
                    grad_all.at[middle + sign * step, :, sub_cols[u]],
                    ag_ss.at[way, step - 1, u], ag_rs.at[way, step - 1, u], right if way == 0 else left)

    def grad_arrives(way, step, u):
        grad_copy(way, step, u).wait_recv()

    def grad_start(way, step, u):
        copy = grad_copy(way, step, u)
        copy.start()
        drain.append(copy.wait_send)

    def grad_step(step):
        for u in range(SUBS):
            for way in range(2):
                if step <= far[way]:
                    grad_arrives(way, step, u)
                    if step < far[way]:
                        grad_start(way, step + 1, u)

    for u in range(SUBS):
        for way in range(2):
            grad_start(way, 1, u)

    for h in range(heads):
        for t, ref in enumerate((q_ref, k_ref, v_ref)):
            place = pl.ds(pl.multiple_of(c * span, span), span)

            def copy_of(h=h, t=t, ref=ref, place=place):
                return send(ref.at[0, :, fixed_cols[h]], qkv.at[t, place, :],
                            qkv_ss.at[t, h], qkv_rs.at[t, c], {"col": owner(h)})

            @pl.when(c != owner(h))
            def _(copy_of=copy_of):
                copy_of().start()

            @pl.when(c == owner(h))
            def _(h=h, t=t, ref=ref, place=place):
                qkv[t, place, :] = ref[0, :, fixed_cols[h]]

            def wait_sent(h=h, copy_of=copy_of):
                @pl.when(c != owner(h))
                def _():
                    copy_of().wait_send()

            drain.append(wait_sent)

    block_rows = min(128, length)

    def forward(first, last):
        @pl.when(is_head)
        def _():
            @pl.loop(first, last)
            def _(i):
                at = pl.ds(pl.multiple_of(i * block_rows, block_rows), block_rows)
                logits = lax.dot_general(qkv[0, at, :], qkv[1], NT, preferred_element_type=F32)
                visible = pos_ref[...].astype(F32) <= pos_col[at, 0:1]
                logits = jnp.where(visible, logits * scale, -jnp.inf)
                highest = jnp.max(logits, axis=-1, keepdims=True)
                grown = jnp.exp(logits - highest)
                prob = grown / jnp.sum(grown, axis=-1, keepdims=True)
                probs[at, :] = prob
                rounded = prob.astype(BF16)
                probs_b[at, :] = rounded
                context = jnp.dot(rounded, qkv[2], preferred_element_type=F32)
                ctx_own[at, :] = context.astype(BF16)

    n_blocks = length // block_rows

    def heads_arrive():
        @pl.when(is_head)
        def _():
            pos_col[...] = jnp.transpose(
                jnp.broadcast_to(pos_ref[...].astype(F32), (128, length))
            )
            for i in range(1, n_col):
                src = lax.rem(c + i, n_col)
                for t in range(3):
                    place = qkv.at[t, pl.ds(pl.multiple_of(src * span, span), span), :]
                    send(place, place, qkv_ss.at[t, 0], qkv_rs.at[t, src], {"col": src}).wait_recv()

    half_rows = length // 2

    def ctx_rows(half):
        place = b if half == 0 else 1 - b
        return pl.ds(pl.multiple_of(place * length, length), length)

    def cross_copy(way):
        return send(ctx_own.at[pl.ds(way * half_rows, half_rows), :], relay.at[way],
                    cross_ss.at[0, way], cross_rs.at[0, way], right if way == 0 else left)

    def relay_copy(way):
        origin = lax.div(chunk_at(-1 if way == 0 else 1), n_row)
        at = pl.ds(pl.multiple_of(origin * length + way * half_rows, half_rows), half_rows)
        return send(relay.at[way], ctx_all.at[at, head_cols],
                    cross_ss.at[1, way], cross_rs.at[1, way], far_right if way == 0 else far_left)

    def cross_arrives(way):
        at = pl.ds(pl.multiple_of((1 - b) * length + way * half_rows, half_rows), half_rows)
        block = ctx_all.at[at, head_cols]
        send(block, block, cross_ss.at[1, way], cross_rs.at[1, way], far_right).wait_recv()

    def ctx_copies(half):
        src = ctx_own if half == 0 else ctx_all.at[ctx_rows(1), head_cols]
        targets = [sibling] + [{"col": lax.rem(c + 2 * i, n_col)} for i in range(1, n_col // 2)]
        return [
            send(src, ctx_all.at[ctx_rows(half), head_cols], ctx_ss.at[half, i], ctx_rs.at[half, head], to)
            for i, to in enumerate(targets)
        ]

    def ctx_block(half, h):
        block = ctx_all.at[ctx_rows(half), fixed_cols[h]]
        return send(block, block, fwd_ss.at[half, h], ctx_rs.at[half, h], sibling)

    def passes_on(h):
        return jnp.logical_and(core == owner(h) % 2, c != owner(h))

    def ctx_forward(half):
        for h in range(heads):
            @pl.when(passes_on(h))
            def _(h=h):
                ctx_block(half, h).wait_recv()
                ctx_block(half, h).start()

    def ctx_wait(half):
        for h in range(heads):
            @pl.when(core != owner(h) % 2)
            def _(h=h):
                ctx_block(half, h).wait_recv()

    def cross_start():
        @pl.when(is_head)
        def _():
            for way in range(2):
                cross_copy(way).start()

    def ctx_start():
        @pl.when(is_head)
        def _():
            for copy in ctx_copies(0):
                copy.start()
            ctx_all[ctx_rows(0), head_cols] = ctx_own[...]

    def cross_relay():
        @pl.when(is_head)
        def _():
            for way in range(2):
                cross_copy(way).wait_recv()
                relay_copy(way).start()

    def cross_finish():
        @pl.when(is_head)
        def _():
            for way in range(2):
                cross_arrives(way)
            for copy in ctx_copies(1):
                copy.start()

    def ctx_in_order():
        for slot in range(ring):
            held = chunk_at(slot - middle)
            ctx_rel[slot * rows:(slot + 1) * rows, :] = ctx_all[pl.ds(pl.multiple_of(held * rows, rows), rows), :]

    def ctx_drain():
        @pl.when(is_head)
        def _():
            for way in range(2):
                cross_copy(way).wait_send()
                relay_copy(way).wait_send()
            for half in range(2):
                for copy in ctx_copies(half):
                    copy.wait_send()
        for half in range(2):
            for h in range(heads):
                @pl.when(passes_on(h))
                def _(h=h, half=half):
                    ctx_block(half, h).wait_send()

    drain.append(ctx_drain)

    def context_grad(offset):
        block = r + turn * offset

        @pl.when(jnp.logical_and(block >= 0, block < n_row))
        def _():
            held = middle + offset
            place = pl.ds(pl.multiple_of(block * rows, rows), rows)

            @pl.loop(0, heads // 2)
            def _(i):
                two = pl.ds(pl.multiple_of(i * 2 * HEAD_DIM, 2 * HEAD_DIM), 2 * HEAD_DIM)
                product = lax.dot_general(grad_all[held], w_ref[two, :], NT, preferred_element_type=F32)
                cg_stage[place, two] = product.astype(BF16)
                for k in range(2):
                    h = 2 * i + k
                    to = lax.div(h * n_col, heads)
                    own = pl.ds(pl.multiple_of(h * HEAD_DIM, HEAD_DIM), HEAD_DIM)

                    @pl.when(c != to)
                    def _(h=h, to=to, own=own):
                        send(cg_stage.at[place, own], cg_recv.at[c, place, :], cg_ss.at[h], cg_rs.at[c], {"col": to}).start()

                    @pl.when(c == to)
                    def _(k=k):
                        cg_recv[c, place, :] = product[:, k * HEAD_DIM:(k + 1) * HEAD_DIM].astype(BF16)

    def context_grads(step):
        if step == 0:
            context_grad(0)
        elif step < n_row:
            @pl.loop(0, 2)
            def _(way):
                context_grad((2 * way - 1) * step)

    def cg_drain():
        for h in range(heads):
            @pl.when(c != owner(h))
            def _(h=h):
                wait_bytes(cg_recv.at[0], cg_ss.at[h])

    drain.append(cg_drain)

    tile = cols // 3

    def project(first, last):
        tokens = ctx_rel[(middle - reach + first) * rows:(middle - reach + last) * rows, :]

        @pl.loop(0, 3)
        def _(i):
            at = pl.ds(pl.multiple_of(i * tile, tile), tile)
            product = jnp.dot(tokens, w_ref[:, at], preferred_element_type=F32)
            lo[first:last, :, at] = product.reshape(last - first, rows, tile)

    def project_ends():
        project(0, 2)
        if reach > 1:
            project(2 * reach - 2, 2 * reach)

    def project_middle():
        if reach > 2:
            project(2, 2 * reach - 2)

    def out_step(way, step, final=False):
        stage, landed = (rs_stage_r, rs_r) if way == 0 else (rs_stage_l, rs_l)
        place = (2 * reach - step) if way == 0 else step - 1
        for u in range(SUBS):
            total = lo[place, :, sub_cols[u]]
            if step > 1:
                block = landed.at[step - 2, :, sub_cols[u]]
                send(block, block, rs_ss.at[way, step - 2, u], rs_rs.at[way, step - 2, u], right).wait_recv()
                total = total + block[...].astype(F32)
            if final:
                lo[place, :, sub_cols[u]] = total
                continue
            stage[step - 1, :, sub_cols[u]] = total.astype(BF16)
            copy = send(stage.at[step - 1, :, sub_cols[u]], landed.at[step - 1, :, sub_cols[u]],
                        rs_ss.at[way, step - 1, u], rs_rs.at[way, step - 1, u], right if way == 0 else left)
            copy.start()
            drain.append(copy.wait_send)

    def out_both(step):
        if step < reach:
            out_step(0, step)
        if step <= reach:
            out_step(1, step)

    stripe = cols // n_depth
    part = stripe // 2

    def weight_product(place, first, last):
        at = pl.ds(pl.multiple_of(place * 2 * stripe + b * 128, 128), 256)
        tokens = grad_all[first:last, :, at].reshape((last - first) * rows, 256)
        return lax.dot_general(tokens, ctx_rel[first * rows:last * rows, :], TN, preferred_element_type=F32)

    def weight_near():
        @pl.loop(0, n_y)
        def _(place):
            dw_sum[place] = weight_product(place, middle - reach, middle + reach)

    def weight_far(place):
        place = lax.rem(place + 2 * n_y, n_y)
        dw_sum[place] += weight_product(place, 0, middle - reach) + weight_product(place, middle + reach, ring)

    def weight_step(way, step, final=False):
        place = lax.rem(y + (-step if way == 0 else step) + 2 * n_y, n_y)
        own = slice(way * part, (way + 1) * part)
        total = dw_sum[place, pl.ds(pl.multiple_of(b * 64 + way * part, 32), part), :]
        if step > 1:
            block = dw_recv.at[way, step - 2]
            send(block, block, dw_ss.at[way, step - 2], dw_rs.at[way, step - 2], up).wait_recv()
            total = total + block[...].astype(F32)
        if final:
            dw_ref[own, :] = total
            return
        dw_stage[way, step - 1] = total.astype(BF16)
        copy = send(dw_stage.at[way, step - 1], dw_recv.at[way, step - 1], dw_ss.at[way, step - 1],
                    dw_rs.at[way, step - 1], up if way == 0 else down)
        copy.start()
        drain.append(copy.wait_send)

    def backward():
        @pl.when(is_head)
        def _():
            for i in range(1, n_col):
                src = lax.rem(c + i, n_col)
                wait_bytes(cg_recv.at[src], cg_rs.at[src])

            @pl.loop(0, n_blocks)
            def _(i):
                at = pl.ds(pl.multiple_of(i * block_rows, block_rows), block_rows)
                total = cg_recv[0, at, :].astype(F32)
                for k in range(1, n_col):
                    total = total + cg_recv[k, at, :].astype(F32)
                grad = total.astype(BF16)
                cg_own[at, :] = grad
                row_dot = jnp.sum(grad.astype(F32) * ctx_own[at, :].astype(F32), axis=-1, keepdims=True)
                dprob = lax.dot_general(grad, qkv[2], NT, preferred_element_type=F32)
                rounded = (probs[at, :] * (dprob - row_dot)).astype(BF16)
                dlogits[at, :] = rounded
                query_grad = jnp.dot(rounded, qkv[1], preferred_element_type=F32) * scale
                dqkv_own[0, at, :] = query_grad.astype(BF16)

            key_grad = lax.dot_general(dlogits[...], qkv[0], TN, preferred_element_type=F32) * scale
            dqkv_own[1] = key_grad.astype(BF16)
            value_grad = lax.dot_general(probs_b[...], cg_own[...], TN, preferred_element_type=F32)
            dqkv_own[2] = value_grad.astype(BF16)
            for t in range(3):
                for i in range(1, n_col):
                    dqkv_copy(t, i).start()
                dqkv_all[t, :, head_cols] = dqkv_own[t, pl.ds(pl.multiple_of(c * span, span), span), :]

    def dqkv_copy(t, i):
        to = lax.rem(c + i, n_col)
        return send(dqkv_own.at[t, pl.ds(pl.multiple_of(to * span, span), span), :],
                    dqkv_all.at[t, :, head_cols], dq_ss.at[t, i], dq_rs.at[t, head], {"col": to})

    def dqkv_drain():
        @pl.when(is_head)
        def _():
            for t in range(3):
                for i in range(1, n_col):
                    dqkv_copy(t, i).wait_send()

    drain.append(dqkv_drain)

    def weight_ends():
        for way in range(2):
            if n_y > 2 or way == 0:
                weight_far(y + 2 * way - 1)
            weight_step(way, 1)

    def weight_rest():
        for offset in range(2, n_y - 1):
            weight_far(y + offset)
        weight_far(y)

    def weight_both(step):
        if step < n_y:
            weight_step(0, step)
            weight_step(1, step)

    grad_step(1)
    heads_arrive()
    forward(0, n_blocks // 2)
    grad_step(2)
    forward(n_blocks // 2, n_blocks)
    cross_start()
    cross_relay()
    ctx_start()
    weight_copy.wait()
    context_grads(0)
    context_grads(1)
    grad_step(3)
    context_grads(2)
    grad_step(4)
    ctx_forward(0)
    context_grads(3)
    grad_step(5)
    ctx_wait(0)
    cross_finish()
    context_grads(4)
    grad_step(6)
    context_grads(5)
    ctx_forward(1)
    grad_step(7)
    context_grads(6)
    context_grads(7)
    ctx_wait(1)
    ctx_in_order()
    project_ends()
    grad_step(8)
    out_both(1)
    project_middle()
    weight_near()
    out_both(2)
    weight_ends()
    weight_rest()
    out_both(3)
    weight_both(2)
    backward()
    out_both(4)
    weight_both(3)
    out_step(0, reach, final=True)
    out_step(1, reach + 1, final=True)
    out_ref[0] = lo[reach].astype(BF16)
    weight_step(0, n_y, final=True)
    weight_step(1, n_y, final=True)
    for t, ref in enumerate((dq_ref, dk_ref, dv_ref)):
        for h in range(heads):
            @pl.when(c != owner(h))
            def _(t=t, h=h):
                block = dqkv_all.at[t, :, fixed_cols[h]]
                send(block, block, dq_ss.at[t, 0], dq_rs.at[t, h], sibling).wait_recv()
        ref[0] = dqkv_all[t]
    for wait in drain:
        wait()


def hand_over(*refs):
    count = len(refs) // 2
    *refs, sem = refs
    copies = [pltpu.make_async_copy(refs[i], refs[count + i], sem.at[i]) for i in range(count)]
    for copy in copies:
        copy.start()
    for copy in copies:
        copy.wait()


def solution(mesh):
    n_row, n_col, n_depth = mesh.shape["row"], mesh.shape["col"], mesh.shape["depth"]

    def local(q, k, v, positions, weight, grad):
        _, span, width = q.shape
        _, rows, cols = grad.shape
        length = positions.shape[1]
        heads, ring, reach, n_y = width // HEAD_DIM, HALVES * n_row, n_row // 2, n_depth // HALVES
        stripe = cols // n_depth
        vmem = pl.BlockSpec(memory_space=pltpu.VMEM)
        dma = pltpu.SemaphoreType.DMA
        hops, turns = max(reach, 1), max(n_y - 1, 1)
        scratch = [
            pltpu.VMEM((width, cols), BF16),
            pltpu.VMEM((3, length, HEAD_DIM), BF16),
            pltpu.VMEM((length, 128), F32),
            pltpu.VMEM((length, length), F32),
            pltpu.VMEM((length, length), BF16),
            pltpu.VMEM((length, length), BF16),
            pltpu.VMEM((length, HEAD_DIM), BF16),
            pltpu.VMEM((HALVES * length, width), BF16),
            pltpu.VMEM((HALVES * length, width), BF16),
            pltpu.VMEM((2, length // 2, HEAD_DIM), BF16),
            pltpu.VMEM((ring, rows, cols), BF16),
            pltpu.VMEM((length, width), BF16),
            pltpu.VMEM((n_col, length, HEAD_DIM), BF16),
            pltpu.VMEM((length, HEAD_DIM), BF16),
            pltpu.VMEM((3, length, HEAD_DIM), BF16),
            pltpu.VMEM((3, span, width), BF16),
            pltpu.VMEM((2 * reach, rows, cols), F32),
            pltpu.VMEM((hops, rows, cols), BF16),
            pltpu.VMEM((hops, rows, cols), BF16),
            pltpu.VMEM((hops, rows, cols), BF16),
            pltpu.VMEM((hops, rows, cols), BF16),
            pltpu.VMEM((n_y, 256, width), F32),
            pltpu.VMEM((2, turns, stripe // 2, width), BF16),
            pltpu.VMEM((2, turns, stripe // 2, width), BF16),
            dma,
            dma((3, heads)), dma((3, n_col)),
            dma((2, ring // 2, SUBS)), dma((2, ring // 2, SUBS)),
            dma((2, n_col)), dma((2, heads)), dma((2, heads)), dma((2, 2)), dma((2, 2)),
            dma((heads,)), dma((n_col,)),
            dma((3, n_col)), dma((3, heads)),
            dma((2, hops, SUBS)), dma((2, hops, SUBS)),
            dma((2, turns)), dma((2, turns)),
        ]
        parts = pl.pallas_call(
            functools.partial(kernel, n_row, n_col, n_depth),
            out_shape=(
                jax.ShapeDtypeStruct(grad.shape, BF16),
                jax.ShapeDtypeStruct(q.shape, BF16),
                jax.ShapeDtypeStruct(k.shape, BF16),
                jax.ShapeDtypeStruct(v.shape, BF16),
                jax.ShapeDtypeStruct((stripe, width), F32),
            ),
            in_specs=[vmem] * 4 + [pl.BlockSpec(memory_space=pl.ANY), vmem],
            out_specs=(vmem,) * 5,
            scratch_shapes=scratch,
            compiler_params=pltpu.CompilerParams(
                collective_id=0, has_side_effects=True, vmem_limit_bytes=VMEM_BYTES
            ),
        )(q, k, v, positions, weight, grad)
        anywhere = pl.BlockSpec(memory_space=pltpu.HBM)
        *parts, weight_grad = pl.pallas_call(
            hand_over,
            out_shape=[jax.ShapeDtypeStruct(part.shape, part.dtype) for part in parts],
            in_specs=[anywhere] * len(parts),
            out_specs=[anywhere] * len(parts),
            scratch_shapes=[dma((len(parts),))],
            compiler_params=pltpu.CompilerParams(vmem_limit_bytes=VMEM_BYTES),
        )(*parts)
        return *parts, weight_grad.T

    return jax.shard_map(
        local,
        mesh=mesh,
        in_specs=(
            P("depth", "col", "row"),
            P("depth", "col", "row"),
            P("depth", "col", "row"),
            P("depth", None),
            P("row", "col"),
            P("depth", "row", "col"),
        ),
        out_specs=(
            P("depth", "row", "col"),
            P("depth", "col", "row"),
            P("depth", "col", "row"),
            P("depth", "col", "row"),
            P("row", ("col", "depth")),
        ),
        check_vma=False,
    )
```

```python
import functools

import jax
import jax.numpy as jnp
from jax import lax
from jax.experimental import pallas as pl
from jax.experimental.pallas import tpu as pltpu
from jax.sharding import PartitionSpec as P

HEAD_DIM = 128
HALVES = 2
THIRDS = 3
SUBS = 2
LANES = 128
VMEM_BYTES = 56 * 1024 * 1024
MESH = pl.DeviceIdType.MESH
F32, BF16 = jnp.float32, jnp.bfloat16

NT = (((1,), (1,)), ((), ()))
TN = (((0,), (0,)), ((), ()))


def kernel(
    n_row, n_col, n_depth,
    q_ref, k_ref, v_ref, pos_ref, w_hbm, g_ref,
    out_ref, dq_ref, dk_ref, dv_ref, dw_ref,
    w_ref, qkv_stage, qkv, pos_col, probs, probs_b, dlogits, ctx_own, ctx_all, ctx_rel, relay, grad_all,
    cg_stage, cg_recv, cg_near, cg_own, dqkv_own, dqkv_all,
    lo, rs_stage_r, rs_stage_l, rs_r, rs_l, dw_sum, dw_stage, dw_recv,
    w_sem, qkv_ss, qkv_rs, ag_ss, ag_rs, ctx_ss, ctx_rs, fwd_ss, cross_ss, cross_rs, cg_ss, cg_rs, cgx_ss, cgx_rs, dq_ss, dq_rs,
    rs_ss, rs_rs, dw_ss, dw_rs,
):
    r, c, d = lax.axis_index("row"), lax.axis_index("col"), lax.axis_index("depth")
    y, b = lax.div(d, HALVES), lax.rem(d, HALVES)
    ring, n_y = HALVES * n_row, n_depth // HALVES
    reach = n_row // 2
    z = b * n_row + r
    span, width = q_ref.shape[1:]
    rows, cols = g_ref.shape[1:]
    length = pos_ref.shape[1]
    heads = width // HEAD_DIM
    scale = HEAD_DIM ** (-0.5)

    def on_ring(place):
        place = lax.rem(place + 2 * ring, ring)
        return {"row": lax.rem(place, n_row), "depth": y * HALVES + lax.div(place, n_row)}

    def on_y(place):
        return {"depth": lax.rem(place + n_y, n_y) * HALVES + b}

    def chunk_at(offset):
        return lax.rem(z + offset + 2 * ring, ring)

    def owner(h):
        return (h * n_col) // heads

    core = lax.rem(c, 2)
    right, left, up, down = on_ring(z + 1), on_ring(z - 1), on_y(y + 1), on_y(y - 1)
    sibling = {"col": c + 1 - 2 * core}
    far_right, far_left, other = on_ring(z + n_row - 1), on_ring(z - n_row + 1), on_ring(z + n_row)
    middle = ring // 2
    head, is_head = 0, c == owner(0)
    for h in range(1, heads):
        head = jnp.where(c >= owner(h), h, head)
        is_head = jnp.logical_or(is_head, c == owner(h))
    head_cols = pl.ds(pl.multiple_of(head * HEAD_DIM, HEAD_DIM), HEAD_DIM)
    fixed_cols = [pl.ds(h * HEAD_DIM, HEAD_DIM) for h in range(heads)]
    sub_cols = [pl.ds(u * (cols // SUBS), cols // SUBS) for u in range(SUBS)]

    def send(src, dst, send_sem, recv_sem, to):
        return pltpu.make_async_remote_copy(
            src_ref=src, dst_ref=dst, send_sem=send_sem, recv_sem=recv_sem,
            device_id=to, device_id_type=MESH,
        )

    def wait_bytes(ref, sem):
        pltpu.make_async_copy(ref, ref, sem).wait()

    barrier = pltpu.get_barrier_semaphore()
    peers = [{"col": lax.rem(c + i, n_col)} for i in range(1, n_col)]
    peers += [right, left, other, up]
    if n_y > 2:
        peers += [down]
    if n_row > 2:
        peers += [far_right, far_left]
    for peer in peers:
        pl.semaphore_signal(barrier, inc=1, device_id=peer, device_id_type=MESH)
    third = cols // THIRDS
    tiles = [(pl.ds((n * THIRDS + t) * LANES, LANES), pl.ds(t * third + n * LANES, LANES))
             for n in range(n_y) for t in range(THIRDS)]
    weight_copies = [pltpu.make_async_copy(w_hbm.at[:, given], w_ref.at[:, held], w_sem.at[i])
                     for i, (given, held) in enumerate(tiles)]
    for copy in weight_copies:
        copy.start()
    for given, held in tiles:
        grad_all[middle, :, held] = g_ref[0, :, given]
    pl.semaphore_wait(barrier, len(peers))

    drain = []

    far = [ring // 2, ring // 2 - 1]
    near = [reach, reach - 1]
    third_cols = [pl.ds(u * third, third) for u in range(THIRDS)]

    def grad_copy(way, step, u):
        sign = -1 if way == 0 else 1
        return send(grad_all.at[middle + sign * (step - 1), :, third_cols[u]],
                    grad_all.at[middle + sign * step, :, third_cols[u]],
                    ag_ss.at[way, step - 1, u], ag_rs.at[way, step - 1, u], right if way == 0 else left)

    def where_needed(place, way, step, u, action):
        if step <= near[way] or u == 1:
            action()
            return
        place = lax.rem(place + ring, ring)
        line, half = lax.rem(place, n_row), lax.div(place, n_row)
        onward = far[way] - step
        crosses = line + onward >= n_row if way == 0 else line - onward < 0
        pl.when(jnp.logical_or(crosses, half == (0 if u == 0 else 1)))(action)

    def grad_start(way, step, u):
        where_needed(z + (1 if way == 0 else -1), way, step, u, grad_copy(way, step, u).start)

    def grad_step(step):
        for u in (1, 0, 2):
            for way in range(2):
                if step <= far[way]:
                    def pass_on(way=way, u=u):
                        grad_copy(way, step, u).wait_recv()
                        if step < far[way]:
                            grad_start(way, step + 1, u)

                    where_needed(z, way, step, u, pass_on)

    def grad_drain():
        for way in range(2):
            for step in range(1, far[way] + 1):
                for u in range(THIRDS):
                    where_needed(z + (1 if way == 0 else -1), way, step, u, grad_copy(way, step, u).wait_send)

    drain.append(grad_drain)
    for u in (1, 0, 2):
        for way in range(2):
            grad_start(way, 1, u)

    own_span = pl.ds(pl.multiple_of(c * span, span), span)
    for t, ref in enumerate((q_ref, k_ref, v_ref)):
        qkv_stage[t] = ref[0]

    def heads_copy(h):
        return send(qkv_stage.at[:, :, fixed_cols[h]], qkv.at[:, own_span, :],
                    qkv_ss.at[h], qkv_rs.at[c], {"col": owner(h)})

    for h in range(heads):
        @pl.when(c != owner(h))
        def _(h=h):
            heads_copy(h).start()

    @pl.when(is_head)
    def _():
        for t in range(3):
            qkv[t, own_span, :] = qkv_stage[t, :, head_cols]

    def heads_drain():
        for h in range(heads):
            @pl.when(c != owner(h))
            def _(h=h):
                heads_copy(h).wait_send()

    drain.append(heads_drain)

    block_rows = min(128, length)

    def forward(first, last):
        @pl.when(is_head)
        def _():
            for i in range(first, last):
                at = pl.ds(i * block_rows, block_rows)
                logits = lax.dot_general(qkv[0, at, :], qkv[1], NT, preferred_element_type=F32)
                visible = pos_ref[...].astype(F32) <= pos_col[at, 0:1]
                logits = jnp.where(visible, logits * scale, -jnp.inf)
                highest = jnp.max(logits, axis=-1, keepdims=True)
                grown = jnp.exp(logits - highest)
                prob = grown / jnp.sum(grown, axis=-1, keepdims=True)
                probs[at, :] = prob
                rounded = prob.astype(BF16)
                probs_b[at, :] = rounded
                context = jnp.dot(rounded, qkv[2], preferred_element_type=F32)
                ctx_own[at, :] = context.astype(BF16)

    n_blocks = length // block_rows

    def heads_arrive():
        @pl.when(is_head)
        def _():
            pos_col[...] = jnp.transpose(
                jnp.broadcast_to(pos_ref[...].astype(F32), (128, length))
            )
            for i in range(1, n_col):
                src = lax.rem(c + i, n_col)
                place = qkv.at[:, pl.ds(pl.multiple_of(src * span, span), span), :]
                send(place, place, qkv_ss.at[0], qkv_rs.at[src], {"col": src}).wait_recv()

    half_rows, quarter = length // 2, length // 4

    def ctx_rows(group):
        if group == 0:
            return pl.ds(pl.multiple_of(b * length, length), length)
        return crossing_rows(1 - b, r, group - 1)

    def crossing_rows(place, line, phase):
        start = place * length + jnp.where(line < reach, 1 - phase, phase) * half_rows
        return pl.ds(pl.multiple_of(start, half_rows), half_rows)

    def crossing_part(place, line, phase, way):
        start = place * length + jnp.where(line < reach, 1 - phase, phase) * half_rows + way * quarter
        return pl.ds(pl.multiple_of(start, quarter), quarter)

    def cross_copy(phase, way):
        return send(ctx_own.at[crossing_part(0, r, phase, way), :], relay.at[phase, way],
                    cross_ss.at[0, phase, way], cross_rs.at[0, phase, way], right if way == 0 else left)

    def relay_copy(phase, way):
        origin = chunk_at(-1 if way == 0 else 1)
        at = crossing_part(lax.div(origin, n_row), lax.rem(origin, n_row), phase, way)
        return send(relay.at[phase, way], ctx_all.at[at, head_cols],
                    cross_ss.at[1, phase, way], cross_rs.at[1, phase, way], far_right if way == 0 else far_left)

    def cross_arrives(phase, way):
        block = ctx_all.at[crossing_part(1 - b, r, phase, way), head_cols]
        send(block, block, cross_ss.at[1, phase, way], cross_rs.at[1, phase, way], far_right).wait_recv()

    def ctx_copies(group):
        src = ctx_own if group == 0 else ctx_all.at[ctx_rows(group), head_cols]
        targets = [sibling] + [{"col": lax.rem(c + 2 * i, n_col)} for i in range(1, n_col // 2)]
        return [
            send(src, ctx_all.at[ctx_rows(group), head_cols], ctx_ss.at[group, i], ctx_rs.at[group, head], to)
            for i, to in enumerate(targets)
        ]

    def ctx_block(half, h):
        block = ctx_all.at[ctx_rows(half), fixed_cols[h]]
        return send(block, block, fwd_ss.at[half, h], ctx_rs.at[half, h], sibling)

    def passes_on(h):
        return jnp.logical_and(core == owner(h) % 2, c != owner(h))

    def ctx_forward(half):
        for h in range(heads):
            @pl.when(passes_on(h))
            def _(h=h):
                ctx_block(half, h).wait_recv()
                ctx_block(half, h).start()

    def ctx_wait(half):
        for h in range(heads):
            @pl.when(core != owner(h) % 2)
            def _(h=h):
                ctx_block(half, h).wait_recv()

    def cross_start():
        @pl.when(is_head)
        def _():
            for phase in range(2):
                for way in range(2):
                    cross_copy(phase, way).start()

    def ctx_start():
        @pl.when(is_head)
        def _():
            for copy in ctx_copies(0):
                copy.start()
            ctx_all[ctx_rows(0), head_cols] = ctx_own[...]

    def cross_relay():
        @pl.when(is_head)
        def _():
            for phase in range(2):
                for way in range(2):
                    cross_copy(phase, way).wait_recv()
                    relay_copy(phase, way).start()

    def cross_finish(phase):
        @pl.when(is_head)
        def _():
            for way in range(2):
                cross_arrives(phase, way)
            for copy in ctx_copies(1 + phase):
                copy.start()

    def ctx_in_order(first, last):
        for slot in range(first, last):
            held = chunk_at(slot - middle)
            ctx_rel[slot * rows:(slot + 1) * rows, :] = ctx_all[pl.ds(pl.multiple_of(held * rows, rows), rows), :]

    def ctx_drain():
        @pl.when(is_head)
        def _():
            for phase in range(2):
                for way in range(2):
                    cross_copy(phase, way).wait_send()
                    relay_copy(phase, way).wait_send()
            for group in range(3):
                for copy in ctx_copies(group):
                    copy.wait_send()
        for group in range(3):
            for h in range(heads):
                @pl.when(passes_on(h))
                def _(h=h, group=group):
                    ctx_block(group, h).wait_send()

    drain.append(ctx_drain)

    inner = reach // 2
    near_parts = [(reach - inner, 2 * inner), (0, reach - inner), (reach + inner, reach - inner)]

    def near_copy(part, h):
        at = pl.ds(near_parts[part][0] * rows, near_parts[part][1] * rows)
        return send(cg_stage.at[at, fixed_cols[h]], cg_recv.at[c, at, :],
                    cg_ss.at[part, h], cg_rs.at[part, c], {"col": owner(h)})

    def context_grads(parts):
        parts = [part for part in parts if near_parts[part][1] > 0]
        if not parts:
            return
        tokens = []
        for part in parts:
            first, count = near_parts[part]
            slots = grad_all[middle - reach + first:middle - reach + first + count]
            tokens.append(slots.reshape(count * rows, cols))
        tokens = tokens[0] if len(tokens) == 1 else jnp.concatenate(tokens, axis=0)
        for i in range(heads // 2):
            two = pl.ds(i * 2 * HEAD_DIM, 2 * HEAD_DIM)
            product = lax.dot_general(tokens, w_ref[two, :], NT, preferred_element_type=F32).astype(BF16)
            done = 0
            for part in parts:
                first, count = near_parts[part]
                cg_stage[first * rows:(first + count) * rows, two] = product[done:done + count * rows]
                done += count * rows
            for h in (2 * i, 2 * i + 1):
                @pl.when(c != owner(h))
                def _(h=h):
                    for part in parts:
                        near_copy(part, h).start()

    def near_sum():
        @pl.when(is_head)
        def _():
            cg_recv[c] = cg_stage[:, head_cols]
            for i in range(1, n_col):
                src = lax.rem(c + i, n_col)
                for part, (first, count) in enumerate(near_parts):
                    if count > 0:
                        block = cg_recv.at[src, pl.ds(first * rows, count * rows), :]
                        send(block, block, cg_ss.at[part, 0], cg_rs.at[part, src], {"col": src}).wait_recv()
            for i in range(2 * reach):
                at = pl.ds(i * rows, rows)
                total = cg_recv[0, at, :].astype(F32)
                for k in range(1, n_col):
                    total = total + cg_recv[k, at, :].astype(F32)
                cg_near[at, :] = total.astype(BF16)
            for i in range(2 * reach):
                @pl.when(is_own(i))
                def _(i=i):
                    cg_own[near_rows(i), :] = cg_near[i * rows:(i + 1) * rows, :]

                @pl.when(jnp.logical_not(is_own(i)))
                def _(i=i):
                    near_cross(i).start()

    def is_own(i):
        block = r + i - reach
        return jnp.logical_and(block >= 0, block < n_row)

    def near_block(i):
        return lax.rem(r + i - reach + n_row, n_row)

    def near_rows(i):
        return pl.ds(pl.multiple_of(near_block(i) * rows, rows), rows)

    def near_cross(i):
        return send(cg_near.at[pl.ds(i * rows, rows), :], cg_own.at[near_rows(i), :],
                    cgx_ss.at[i], cgx_rs.at[near_block(i)], other)

    def cross_wait():
        for block in range(n_row):
            offset = block - r

            @pl.when(jnp.logical_or(offset < -reach, offset >= reach))
            def _(block=block):
                at = cg_own.at[pl.ds(block * rows, rows), :]
                send(at, at, cgx_ss.at[0], cgx_rs.at[block], other).wait_recv()

    def cg_drain():
        for part, (_, count) in enumerate(near_parts):
            if count > 0:
                for h in range(heads):
                    @pl.when(c != owner(h))
                    def _(part=part, h=h):
                        near_copy(part, h).wait_send()
        for i in range(2 * reach):
            @pl.when(jnp.logical_and(is_head, jnp.logical_not(is_own(i))))
            def _(i=i):
                near_cross(i).wait_send()

    drain.append(cg_drain)

    tile = cols // 3

    def project(first, last):
        tokens = ctx_rel[(middle - reach + first) * rows:(middle - reach + last) * rows, :]

        @pl.loop(0, 3)
        def _(i):
            at = pl.ds(pl.multiple_of(i * tile, tile), tile)
            product = jnp.dot(tokens, w_ref[:, at], preferred_element_type=F32)
            lo[first:last, :, at] = product.reshape(last - first, rows, tile)

    def project_ends():
        project(0, 2)
        if reach > 1:
            project(2 * reach - 2, 2 * reach)

    def project_middle():
        if reach > 2:
            project(2, 2 * reach - 2)

    def out_step(way, step, final=False):
        stage, landed = (rs_stage_r, rs_r) if way == 0 else (rs_stage_l, rs_l)
        place = (2 * reach - step) if way == 0 else step - 1
        for u in range(SUBS):
            total = lo[place, :, sub_cols[u]]
            if step > 1:
                block = landed.at[step - 2, :, sub_cols[u]]
                send(block, block, rs_ss.at[way, step - 2, u], rs_rs.at[way, step - 2, u], right).wait_recv()
                total = total + block[...].astype(F32)
            if final:
                lo[place, :, sub_cols[u]] = total
                continue
            stage[step - 1, :, sub_cols[u]] = total.astype(BF16)
            copy = send(stage.at[step - 1, :, sub_cols[u]], landed.at[step - 1, :, sub_cols[u]],
                        rs_ss.at[way, step - 1, u], rs_rs.at[way, step - 1, u], right if way == 0 else left)
            copy.start()
            drain.append(copy.wait_send)

    def out_both(step):
        if step < reach:
            out_step(0, step)
        if step <= reach:
            out_step(1, step)

    stripe = cols // n_depth
    part = stripe // 2

    def weight_product(place, first, last):
        pair = [
            grad_all[first:last, :, pl.ds(pl.multiple_of((b + i) * third + place * LANES, LANES), LANES)]
            for i in range(2)
        ]
        tokens = jnp.concatenate(pair, axis=-1).reshape((last - first) * rows, 2 * LANES)
        return lax.dot_general(tokens, ctx_rel[first * rows:last * rows, :], TN, preferred_element_type=F32)

    def weight_near(first, last):
        @pl.loop(first, last)
        def _(place):
            dw_sum[place] = weight_product(place, middle - reach, middle + reach)

    def weight_far(place):
        place = lax.rem(place + 2 * n_y, n_y)
        dw_sum[place] += weight_product(place, 0, middle - reach) + weight_product(place, middle + reach, ring)

    def weight_step(way, step, final=False):
        place = lax.rem(y + (-step if way == 0 else step) + 2 * n_y, n_y)
        own = slice(way * part, (way + 1) * part)
        total = dw_sum[place, pl.ds(pl.multiple_of(b * 64 + way * part, 32), part), :]
        if step > 1:
            block = dw_recv.at[way, step - 2]
            send(block, block, dw_ss.at[way, step - 2], dw_rs.at[way, step - 2], up).wait_recv()
            total = total + block[...].astype(F32)
        if final:
            dw_ref[own, :] = total
            return
        dw_stage[way, step - 1] = total.astype(BF16)
        copy = send(dw_stage.at[way, step - 1], dw_recv.at[way, step - 1], dw_ss.at[way, step - 1],
                    dw_rs.at[way, step - 1], up if way == 0 else down)
        copy.start()
        drain.append(copy.wait_send)

    def backward():
        @pl.when(is_head)
        def _():
            cross_wait()
            for i in range(n_blocks):
                at = pl.ds(i * block_rows, block_rows)
                grad = cg_own[at, :]
                row_dot = jnp.sum(grad.astype(F32) * ctx_own[at, :].astype(F32), axis=-1, keepdims=True)
                dprob = lax.dot_general(grad, qkv[2], NT, preferred_element_type=F32)
                rounded = (probs[at, :] * (dprob - row_dot)).astype(BF16)
                dlogits[at, :] = rounded
                query_grad = jnp.dot(rounded, qkv[1], preferred_element_type=F32) * scale
                dqkv_own[0, at, :] = query_grad.astype(BF16)
            key_grad = lax.dot_general(dlogits[...], qkv[0], TN, preferred_element_type=F32) * scale
            dqkv_own[1] = key_grad.astype(BF16)
            value_grad = lax.dot_general(probs_b[...], cg_own[...], TN, preferred_element_type=F32)
            dqkv_own[2] = value_grad.astype(BF16)
            for i in range(1, n_col):
                dqkv_copy(i).start()
            for t in range(3):
                dqkv_all[t, :, head_cols] = dqkv_own[t, own_span, :]

    def dqkv_copy(i):
        to = lax.rem(c + i, n_col)
        return send(dqkv_own.at[:, pl.ds(pl.multiple_of(to * span, span), span), :],
                    dqkv_all.at[:, :, head_cols], dq_ss.at[i], dq_rs.at[head], {"col": to})

    def dqkv_drain():
        @pl.when(is_head)
        def _():
            for i in range(1, n_col):
                dqkv_copy(i).wait_send()

    drain.append(dqkv_drain)

    def weight_ends():
        for way in range(2):
            if n_y > 2 or way == 0:
                weight_far(y + 2 * way - 1)
            weight_step(way, 1)

    def weight_rest():
        for offset in range(2, n_y - 1):
            weight_far(y + offset)
        weight_far(y)

    def weight_both(step):
        if step < n_y:
            weight_step(0, step)
            weight_step(1, step)

    def dqkv_finish():
        for h in range(heads):
            @pl.when(c != owner(h))
            def _(h=h):
                block = dqkv_all.at[:, :, fixed_cols[h]]
                send(block, block, dq_ss.at[0], dq_rs.at[h], sibling).wait_recv()
        for t, ref in enumerate((dq_ref, dk_ref, dv_ref)):
            ref[0] = dqkv_all[t]

    grad_step(1)
    heads_arrive()
    forward(0, n_blocks // 2)
    grad_step(2)
    forward(n_blocks // 2, n_blocks)
    cross_start()
    cross_relay()
    ctx_start()
    cross_finish(0)
    grad_step(3)
    for copy in weight_copies:
        copy.wait()
    context_grads([0])
    ctx_forward(0)
    grad_step(4)
    context_grads([1, 2])
    ctx_wait(0)
    ctx_forward(1)
    grad_step(5)
    ctx_wait(1)
    ctx_in_order(middle - reach, middle + reach)
    project_ends()
    out_both(1)
    weight_near(0, n_y // 2)
    grad_step(6)
    out_both(2)
    project_middle()
    near_sum()
    cross_finish(1)
    grad_step(7)
    ctx_forward(2)
    weight_near(n_y // 2, n_y)
    out_both(3)
    grad_step(8)
    ctx_wait(2)
    ctx_in_order(0, middle - reach)
    ctx_in_order(middle + reach, ring)
    weight_ends()
    weight_rest()
    out_both(4)
    weight_both(2)
    backward()
    weight_both(3)
    out_step(0, reach, final=True)
    out_step(1, reach + 1, final=True)
    for given, held in tiles:
        out_ref[0, :, given] = lo[reach, :, held].astype(BF16)
    weight_step(0, n_y, final=True)
    weight_step(1, n_y, final=True)
    dqkv_finish()
    for wait in drain:
        wait()


def hand_over(*refs):
    count = len(refs) // 3
    parts, outs, held = refs[:count], refs[count:2 * count], refs[2 * count:3 * count]
    sem = refs[-1]
    inward = [pltpu.make_async_copy(parts[i], held[i], sem.at[0, i]) for i in range(count)]
    outward = [pltpu.make_async_copy(held[i], outs[i], sem.at[1, i]) for i in range(count)]
    for copy in inward:
        copy.start()
    for i in range(count):
        inward[i].wait()
        outward[i].start()
    for copy in outward:
        copy.wait()


def solution(mesh):
    n_row, n_col, n_depth = mesh.shape["row"], mesh.shape["col"], mesh.shape["depth"]

    def local(q, k, v, positions, weight, grad):
        _, span, width = q.shape
        _, rows, cols = grad.shape
        length = positions.shape[1]
        heads, ring, reach, n_y = width // HEAD_DIM, HALVES * n_row, n_row // 2, n_depth // HALVES
        stripe = cols // n_depth
        vmem = pl.BlockSpec(memory_space=pltpu.VMEM)
        dma = pltpu.SemaphoreType.DMA
        hops, turns = max(reach, 1), max(n_y - 1, 1)
        scratch = [
            pltpu.VMEM((width, cols), BF16),
            pltpu.VMEM((3, span, width), BF16),
            pltpu.VMEM((3, length, HEAD_DIM), BF16),
            pltpu.VMEM((length, 128), F32),
            pltpu.VMEM((length, length), F32),
            pltpu.VMEM((length, length), BF16),
            pltpu.VMEM((length, length), BF16),
            pltpu.VMEM((length, HEAD_DIM), BF16),
            pltpu.VMEM((HALVES * length, width), BF16),
            pltpu.VMEM((HALVES * length, width), BF16),
            pltpu.VMEM((2, 2, length // 4, HEAD_DIM), BF16),
            pltpu.VMEM((ring, rows, cols), BF16),
            pltpu.VMEM((length, width), BF16),
            pltpu.VMEM((n_col, length, HEAD_DIM), BF16),
            pltpu.VMEM((length, HEAD_DIM), BF16),
            pltpu.VMEM((length, HEAD_DIM), BF16),
            pltpu.VMEM((3, length, HEAD_DIM), BF16),
            pltpu.VMEM((3, span, width), BF16),
            pltpu.VMEM((2 * reach, rows, cols), F32),
            pltpu.VMEM((hops, rows, cols), BF16),
            pltpu.VMEM((hops, rows, cols), BF16),
            pltpu.VMEM((hops, rows, cols), BF16),
            pltpu.VMEM((hops, rows, cols), BF16),
            pltpu.VMEM((n_y, 256, width), F32),
            pltpu.VMEM((2, turns, stripe // 2, width), BF16),
            pltpu.VMEM((2, turns, stripe // 2, width), BF16),
            dma((THIRDS * n_y,)),
            dma((heads,)), dma((n_col,)),
            dma((2, ring // 2, THIRDS)), dma((2, ring // 2, THIRDS)),
            dma((3, n_col)), dma((3, heads)), dma((3, heads)), dma((2, 2, 2)), dma((2, 2, 2)),
            dma((3, heads)), dma((3, n_col)), dma((2 * reach,)), dma((n_row,)),
            dma((n_col,)), dma((heads,)),
            dma((2, hops, SUBS)), dma((2, hops, SUBS)),
            dma((2, turns)), dma((2, turns)),
        ]
        parts = pl.pallas_call(
            functools.partial(kernel, n_row, n_col, n_depth),
            out_shape=(
                jax.ShapeDtypeStruct(grad.shape, BF16),
                jax.ShapeDtypeStruct(q.shape, BF16),
                jax.ShapeDtypeStruct(k.shape, BF16),
                jax.ShapeDtypeStruct(v.shape, BF16),
                jax.ShapeDtypeStruct((stripe, width), F32),
            ),
            in_specs=[vmem] * 4 + [pl.BlockSpec(memory_space=pl.ANY), vmem],
            out_specs=(vmem,) * 5,
            scratch_shapes=scratch,
            compiler_params=pltpu.CompilerParams(
                collective_id=0, has_side_effects=True, vmem_limit_bytes=VMEM_BYTES
            ),
        )(q, k, v, positions, weight, grad)
        anywhere = pl.BlockSpec(memory_space=pltpu.HBM)
        *parts, weight_grad = pl.pallas_call(
            hand_over,
            out_shape=[jax.ShapeDtypeStruct(part.shape, part.dtype) for part in parts],
            in_specs=[anywhere] * len(parts),
            out_specs=[anywhere] * len(parts),
            scratch_shapes=[pltpu.VMEM(part.shape, part.dtype) for part in parts] + [dma((2, len(parts)))],
            compiler_params=pltpu.CompilerParams(vmem_limit_bytes=VMEM_BYTES),
        )(*parts)
        return *parts, weight_grad.T

    return jax.shard_map(
        local,
        mesh=mesh,
        in_specs=(
            P("depth", "col", "row"),
            P("depth", "col", "row"),
            P("depth", "col", "row"),
            P("depth", None),
            P("row", "col"),
            P("depth", "row", "col"),
        ),
        out_specs=(
            P("depth", "row", "col"),
            P("depth", "col", "row"),
            P("depth", "col", "row"),
            P("depth", "col", "row"),
            P("row", ("col", "depth")),
        ),
        check_vma=False,
    )
```

```python
import functools

import jax
import jax.numpy as jnp
from jax import lax
from jax.experimental import pallas as pl
from jax.experimental.pallas import tpu as pltpu
from jax.sharding import PartitionSpec as P

HEAD_DIM = 128
HALVES = 2
THIRDS = 3
SUBS = 2
LANES = 128
VMEM_BYTES = 56 * 1024 * 1024
MESH = pl.DeviceIdType.MESH
F32, BF16 = jnp.float32, jnp.bfloat16

NT = (((1,), (1,)), ((), ()))
TN = (((0,), (0,)), ((), ()))


def kernel(
    n_row, n_col, n_depth,
    q_ref, k_ref, v_ref, pos_ref, w_hbm, g_ref,
    out_ref, dq_ref, dk_ref, dv_ref, dw_ref,
    w_ref, qkv_stage, qkv, pos_col, probs, probs_b, dlogits, ctx_own, ctx_all, ctx_rel, relay, grad_all,
    cg_stage, cg_recv, cg_near, cg_own, dqkv_own, dqkv_all,
    lo, rs_stage_r, rs_stage_l, rs_r, rs_l, dw_sum, dw_stage, dw_recv,
    w_sem, g_sem, in_sem, qkv_ss, qkv_rs, ag_ss, ag_rs, ctx_ss, ctx_rs, cross_ss, cross_rs, cg_ss, cg_rs, cgx_ss, cgx_rs, dq_ss, dq_rs,
    rs_ss, rs_rs, dw_ss, dw_rs,
):
    r, c, d = lax.axis_index("row"), lax.axis_index("col"), lax.axis_index("depth")
    y, b = lax.div(d, HALVES), lax.rem(d, HALVES)
    ring, n_y = HALVES * n_row, n_depth // HALVES
    reach = n_row // 2
    z = b * n_row + r
    span, width = q_ref.shape[1:]
    rows, cols = g_ref.shape[1:]
    length = pos_ref.shape[1]
    heads = width // HEAD_DIM
    scale = HEAD_DIM ** (-0.5)

    def on_ring(place):
        place = lax.rem(place + 2 * ring, ring)
        return {"row": lax.rem(place, n_row), "depth": y * HALVES + lax.div(place, n_row)}

    def on_y(place):
        return {"depth": lax.rem(place + n_y, n_y) * HALVES + b}

    def chunk_at(offset):
        return lax.rem(z + offset + 2 * ring, ring)

    def owner(h):
        return (h * n_col) // heads

    right, left, up, down = on_ring(z + 1), on_ring(z - 1), on_y(y + 1), on_y(y - 1)
    far_right, far_left, other = on_ring(z + n_row - 1), on_ring(z - n_row + 1), on_ring(z + n_row)
    middle = ring // 2
    head, is_head = 0, c == owner(0)
    for h in range(1, heads):
        head = jnp.where(c >= owner(h), h, head)
        is_head = jnp.logical_or(is_head, c == owner(h))
    head_cols = pl.ds(pl.multiple_of(head * HEAD_DIM, HEAD_DIM), HEAD_DIM)
    fixed_cols = [pl.ds(h * HEAD_DIM, HEAD_DIM) for h in range(heads)]
    sub_cols = [pl.ds(u * (cols // SUBS), cols // SUBS) for u in range(SUBS)]

    def send(src, dst, send_sem, recv_sem, to):
        return pltpu.make_async_remote_copy(
            src_ref=src, dst_ref=dst, send_sem=send_sem, recv_sem=recv_sem,
            device_id=to, device_id_type=MESH,
        )

    barrier = pltpu.get_barrier_semaphore()
    peers = [{"col": lax.rem(c + i, n_col)} for i in range(1, n_col)]
    peers += [right, left, other, up]
    if n_y > 2:
        peers += [down]
    if n_row > 2:
        peers += [far_right, far_left]
    for peer in peers:
        pl.semaphore_signal(barrier, inc=1, device_id=peer, device_id_type=MESH)
    third = cols // THIRDS
    tiles = [(pl.ds((n * THIRDS + t) * LANES, LANES), pl.ds(t * third + n * LANES, LANES))
             for n in range(n_y) for t in range(THIRDS)]
    weight_copies = [pltpu.make_async_copy(w_hbm.at[:, given], w_ref.at[:, held], w_sem.at[i])
                     for i, (given, held) in enumerate(tiles)]
    head_copies = [pltpu.make_async_copy(ref.at[0], qkv_stage.at[t], in_sem.at[t])
                   for t, ref in enumerate((q_ref, k_ref, v_ref))]
    grad_copies = [pltpu.make_async_copy(g_ref.at[0, :, given], grad_all.at[middle, :, held], g_sem.at[i])
                   for i, (given, held) in enumerate(tiles)]
    for copy in grad_copies + head_copies + weight_copies:
        copy.start()
    for copy in grad_copies + head_copies:
        copy.wait()
    pl.semaphore_wait(barrier, len(peers))

    drain, late = [], []

    far = [ring // 2, ring // 2 - 1]
    near = [reach, reach - 1]
    third_cols = [pl.ds(u * third, third) for u in range(THIRDS)]

    def grad_copy(way, step, u):
        sign = -1 if way == 0 else 1
        return send(grad_all.at[middle + sign * (step - 1), :, third_cols[u]],
                    grad_all.at[middle + sign * step, :, third_cols[u]],
                    ag_ss.at[way, step - 1, u], ag_rs.at[way, step - 1, u], right if way == 0 else left)

    def where_needed(place, way, step, u, action):
        if step <= near[way] or u == 1:
            action()
            return
        place = lax.rem(place + ring, ring)
        line, half = lax.rem(place, n_row), lax.div(place, n_row)
        onward = far[way] - step
        crosses = line + onward >= n_row if way == 0 else line - onward < 0
        pl.when(jnp.logical_or(crosses, half == (0 if u == 0 else 1)))(action)

    def grad_start(way, step, u):
        where_needed(z + (1 if way == 0 else -1), way, step, u, grad_copy(way, step, u).start)

    def grad_step(step):
        for u in (1, 0, 2):
            for way in range(2):
                if step <= far[way]:
                    def pass_on(way=way, u=u):
                        grad_copy(way, step, u).wait_recv()
                        if step < far[way]:
                            grad_start(way, step + 1, u)

                    where_needed(z, way, step, u, pass_on)

    def grad_drain():
        for way in range(2):
            for step in range(1, far[way] + 1):
                for u in range(THIRDS):
                    where_needed(z + (1 if way == 0 else -1), way, step, u, grad_copy(way, step, u).wait_send)

    drain.append(grad_drain)
    for u in (1, 0, 2):
        for way in range(2):
            grad_start(way, 1, u)

    own_span = pl.ds(pl.multiple_of(c * span, span), span)
    def heads_copy(h):
        return send(qkv_stage.at[:, :, fixed_cols[h]], qkv.at[:, own_span, :],
                    qkv_ss.at[h], qkv_rs.at[c], {"col": owner(h)})

    for h in range(heads):
        @pl.when(c != owner(h))
        def _(h=h):
            heads_copy(h).start()

    @pl.when(is_head)
    def _():
        for t in range(3):
            qkv[t, own_span, :] = qkv_stage[t, :, head_cols]

    def heads_drain():
        for h in range(heads):
            @pl.when(c != owner(h))
            def _(h=h):
                heads_copy(h).wait_send()

    drain.append(heads_drain)

    block_rows = min(128, length)

    def forward(first, last):
        @pl.when(is_head)
        def _():
            for i in range(first, last):
                at = pl.ds(i * block_rows, block_rows)
                logits = lax.dot_general(qkv[0, at, :], qkv[1], NT, preferred_element_type=F32)
                visible = pos_ref[...].astype(F32) <= pos_col[at, 0:1]
                logits = jnp.where(visible, logits * scale, -jnp.inf)
                highest = jnp.max(logits, axis=-1, keepdims=True)
                grown = jnp.exp(logits - highest)
                prob = grown * (1.0 / jnp.sum(grown, axis=-1, keepdims=True))
                probs[at, :] = prob
                rounded = prob.astype(BF16)
                probs_b[at, :] = rounded
                context = jnp.dot(rounded, qkv[2], preferred_element_type=F32)
                ctx_own[at, :] = context.astype(BF16)

    n_blocks = length // block_rows

    def heads_arrive():
        @pl.when(is_head)
        def _():
            pos_col[...] = jnp.transpose(
                jnp.broadcast_to(pos_ref[...].astype(F32), (128, length))
            )
            for i in range(1, n_col):
                src = lax.rem(c + i, n_col)
                place = qkv.at[:, pl.ds(pl.multiple_of(src * span, span), span), :]
                send(place, place, qkv_ss.at[0], qkv_rs.at[src], {"col": src}).wait_recv()

    half_rows, quarter = length // 2, length // 4

    def ctx_rows(group):
        if group == 0:
            return pl.ds(pl.multiple_of(b * length, length), length)
        return crossing_rows(1 - b, r, group - 1)

    def crossing_rows(place, line, phase):
        start = place * length + jnp.where(line < reach, 1 - phase, phase) * half_rows
        return pl.ds(pl.multiple_of(start, half_rows), half_rows)

    def crossing_part(place, line, phase, way):
        start = place * length + jnp.where(line < reach, 1 - phase, phase) * half_rows + way * quarter
        return pl.ds(pl.multiple_of(start, quarter), quarter)

    def cross_copy(phase, way):
        return send(ctx_own.at[crossing_part(0, r, phase, way), :], relay.at[phase, way],
                    cross_ss.at[0, phase, way], cross_rs.at[0, phase, way], right if way == 0 else left)

    def relay_copy(phase, way):
        origin = chunk_at(-1 if way == 0 else 1)
        at = crossing_part(lax.div(origin, n_row), lax.rem(origin, n_row), phase, way)
        return send(relay.at[phase, way], ctx_all.at[at, head_cols],
                    cross_ss.at[1, phase, way], cross_rs.at[1, phase, way], far_right if way == 0 else far_left)

    def cross_arrives(phase, way):
        block = ctx_all.at[crossing_part(1 - b, r, phase, way), head_cols]
        send(block, block, cross_ss.at[1, phase, way], cross_rs.at[1, phase, way], far_right).wait_recv()

    def ctx_copies(group):
        src = ctx_own if group == 0 else ctx_all.at[ctx_rows(group), head_cols]
        targets = [{"col": lax.rem(c + i, n_col)} for i in range(1, n_col)]
        return [
            send(src, ctx_all.at[ctx_rows(group), head_cols], ctx_ss.at[group, i], ctx_rs.at[group, head], to)
            for i, to in enumerate(targets)
        ]

    def ctx_block(half, h):
        block = ctx_all.at[ctx_rows(half), fixed_cols[h]]
        return send(block, block, ctx_ss.at[0, 0], ctx_rs.at[half, h], right)

    def ctx_wait(half):
        for h in range(heads):
            @pl.when(c != owner(h))
            def _(h=h):
                ctx_block(half, h).wait_recv()

    def cross_start():
        @pl.when(is_head)
        def _():
            for phase in range(2):
                for way in range(2):
                    cross_copy(phase, way).start()

    def ctx_start():
        @pl.when(is_head)
        def _():
            for copy in ctx_copies(0):
                copy.start()
            ctx_all[ctx_rows(0), head_cols] = ctx_own[...]

    def cross_relay():
        @pl.when(is_head)
        def _():
            for phase in range(2):
                for way in range(2):
                    cross_copy(phase, way).wait_recv()
                    relay_copy(phase, way).start()

    def cross_finish(phase):
        @pl.when(is_head)
        def _():
            for way in range(2):
                cross_arrives(phase, way)
            for copy in ctx_copies(1 + phase):
                copy.start()

    def ctx_in_order(first, last):
        for slot in range(first, last):
            held = chunk_at(slot - middle)
            ctx_rel[slot * rows:(slot + 1) * rows, :] = ctx_all[pl.ds(pl.multiple_of(held * rows, rows), rows), :]

    def ctx_drain():
        @pl.when(is_head)
        def _():
            for phase in range(2):
                for way in range(2):
                    cross_copy(phase, way).wait_send()
                    relay_copy(phase, way).wait_send()
            for group in range(3):
                for copy in ctx_copies(group):
                    copy.wait_send()
    drain.append(ctx_drain)

    inner = reach // 2
    near_parts = [(reach - inner, 2 * inner), (0, reach - inner), (reach + inner, reach - inner)]

    def near_copy(part, h):
        at = pl.ds(near_parts[part][0] * rows, near_parts[part][1] * rows)
        return send(cg_stage.at[at, fixed_cols[h]], cg_recv.at[c, at, :],
                    cg_ss.at[part, h], cg_rs.at[part, c], {"col": owner(h)})

    def context_grads(parts):
        parts = [part for part in parts if near_parts[part][1] > 0]
        if not parts:
            return
        tokens = []
        for part in parts:
            first, count = near_parts[part]
            slots = grad_all[middle - reach + first:middle - reach + first + count]
            tokens.append(slots.reshape(count * rows, cols))
        tokens = tokens[0] if len(tokens) == 1 else jnp.concatenate(tokens, axis=0)
        for i in range(heads // 2):
            two = pl.ds(i * 2 * HEAD_DIM, 2 * HEAD_DIM)
            product = lax.dot_general(tokens, w_ref[two, :], NT, preferred_element_type=F32).astype(BF16)
            done = 0
            for part in parts:
                first, count = near_parts[part]
                cg_stage[first * rows:(first + count) * rows, two] = product[done:done + count * rows]
                done += count * rows
            for h in (2 * i, 2 * i + 1):
                @pl.when(c != owner(h))
                def _(h=h):
                    for part in parts:
                        near_copy(part, h).start()

    def near_sum():
        @pl.when(is_head)
        def _():
            cg_recv[c] = cg_stage[:, head_cols]
            for i in range(1, n_col):
                src = lax.rem(c + i, n_col)
                for part, (first, count) in enumerate(near_parts):
                    if count > 0:
                        block = cg_recv.at[src, pl.ds(first * rows, count * rows), :]
                        send(block, block, cg_ss.at[part, 0], cg_rs.at[part, src], {"col": src}).wait_recv()
            for i in range(2 * reach):
                at = pl.ds(i * rows, rows)
                total = cg_recv[0, at, :].astype(F32)
                for k in range(1, n_col):
                    total = total + cg_recv[k, at, :].astype(F32)
                cg_near[at, :] = total.astype(BF16)
            for i in range(2 * reach):
                @pl.when(is_own(i))
                def _(i=i):
                    cg_own[near_rows(i), :] = cg_near[i * rows:(i + 1) * rows, :]

                @pl.when(jnp.logical_not(is_own(i)))
                def _(i=i):
                    near_cross(i).start()

    def is_own(i):
        block = r + i - reach
        return jnp.logical_and(block >= 0, block < n_row)

    def near_block(i):
        return lax.rem(r + i - reach + n_row, n_row)

    def near_rows(i):
        return pl.ds(pl.multiple_of(near_block(i) * rows, rows), rows)

    def near_cross(i):
        return send(cg_near.at[pl.ds(i * rows, rows), :], cg_own.at[near_rows(i), :],
                    cgx_ss.at[i], cgx_rs.at[near_block(i)], other)

    def cross_wait():
        for block in range(n_row):
            offset = block - r

            @pl.when(jnp.logical_or(offset < -reach, offset >= reach))
            def _(block=block):
                at = cg_own.at[pl.ds(block * rows, rows), :]
                send(at, at, cgx_ss.at[0], cgx_rs.at[block], other).wait_recv()

    def cg_drain():
        for part, (_, count) in enumerate(near_parts):
            if count > 0:
                for h in range(heads):
                    @pl.when(c != owner(h))
                    def _(part=part, h=h):
                        near_copy(part, h).wait_send()
        for i in range(2 * reach):
            @pl.when(jnp.logical_and(is_head, jnp.logical_not(is_own(i))))
            def _(i=i):
                near_cross(i).wait_send()

    drain.append(cg_drain)

    tile = cols // 3

    def project(first, last):
        tokens = ctx_rel[(middle - reach + first) * rows:(middle - reach + last) * rows, :]

        @pl.loop(0, 3)
        def _(i):
            at = pl.ds(pl.multiple_of(i * tile, tile), tile)
            product = jnp.dot(tokens, w_ref[:, at], preferred_element_type=F32)
            lo[first:last, :, at] = product.reshape(last - first, rows, tile)

    def project_ends():
        project(0, 2)
        if reach > 1:
            project(2 * reach - 2, 2 * reach)

    def project_middle():
        if reach > 2:
            project(2, 2 * reach - 2)

    def out_step(way, step, final=False):
        stage, landed = (rs_stage_r, rs_r) if way == 0 else (rs_stage_l, rs_l)
        place = (2 * reach - step) if way == 0 else step - 1
        for u in range(SUBS):
            total = lo[place, :, sub_cols[u]]
            if step > 1:
                block = landed.at[step - 2, :, sub_cols[u]]
                send(block, block, rs_ss.at[way, step - 2, u], rs_rs.at[way, step - 2, u], right).wait_recv()
                total = total + block[...].astype(F32)
            if final:
                lo[place, :, sub_cols[u]] = total
                continue
            stage[step - 1, :, sub_cols[u]] = total.astype(BF16)
            copy = send(stage.at[step - 1, :, sub_cols[u]], landed.at[step - 1, :, sub_cols[u]],
                        rs_ss.at[way, step - 1, u], rs_rs.at[way, step - 1, u], right if way == 0 else left)
            copy.start()
            (drain if step < 3 else late).append(copy.wait_send)

    def out_both(step):
        if step < reach:
            out_step(0, step)
        if step <= reach:
            out_step(1, step)

    stripe = cols // n_depth
    part = stripe // 2

    def weight_product(place, first, last):
        pair = [
            grad_all[first:last, :, pl.ds(pl.multiple_of((b + i) * third + place * LANES, LANES), LANES)]
            for i in range(2)
        ]
        tokens = jnp.concatenate(pair, axis=-1).reshape((last - first) * rows, 2 * LANES)
        return lax.dot_general(tokens, ctx_rel[first * rows:last * rows, :], TN, preferred_element_type=F32)

    def weight_near(first, last):
        @pl.loop(first, last)
        def _(place):
            dw_sum[place] = weight_product(place, middle - reach, middle + reach)

    def weight_far(place):
        place = lax.rem(place + 2 * n_y, n_y)
        dw_sum[place] += weight_product(place, 0, middle - reach) + weight_product(place, middle + reach, ring)

    def weight_step(way, step, final=False):
        place = lax.rem(y + (-step if way == 0 else step) + 2 * n_y, n_y)
        own = slice(way * part, (way + 1) * part)
        total = dw_sum[place, pl.ds(pl.multiple_of(b * 64 + way * part, 32), part), :]
        if step > 1:
            block = dw_recv.at[way, step - 2]
            send(block, block, dw_ss.at[way, step - 2], dw_rs.at[way, step - 2], up).wait_recv()
            total = total + block[...].astype(F32)
        if final:
            dw_ref[own, :] = total
            return
        dw_stage[way, step - 1] = total.astype(BF16)
        copy = send(dw_stage.at[way, step - 1], dw_recv.at[way, step - 1], dw_ss.at[way, step - 1],
                    dw_rs.at[way, step - 1], up if way == 0 else down)
        copy.start()
        late.append(copy.wait_send)

    def backward():
        @pl.when(is_head)
        def _():
            cross_wait()
            for i in range(n_blocks):
                at = pl.ds(i * block_rows, block_rows)
                grad = cg_own[at, :]
                row_dot = jnp.sum(grad.astype(F32) * ctx_own[at, :].astype(F32), axis=-1, keepdims=True)
                dprob = lax.dot_general(grad, qkv[2], NT, preferred_element_type=F32)
                rounded = (probs[at, :] * (dprob - row_dot)).astype(BF16)
                dlogits[at, :] = rounded
                query_grad = jnp.dot(rounded, qkv[1], preferred_element_type=F32) * scale
                dqkv_own[0, at, :] = query_grad.astype(BF16)
            key_grad = lax.dot_general(dlogits[...], qkv[0], TN, preferred_element_type=F32) * scale
            dqkv_own[1] = key_grad.astype(BF16)
            value_grad = lax.dot_general(probs_b[...], cg_own[...], TN, preferred_element_type=F32)
            dqkv_own[2] = value_grad.astype(BF16)
            for i in range(1, n_col):
                dqkv_copy(i).start()
            for t in range(3):
                dqkv_all[t, :, head_cols] = dqkv_own[t, own_span, :]

    def dqkv_copy(i):
        to = lax.rem(c + i, n_col)
        return send(dqkv_own.at[:, pl.ds(pl.multiple_of(to * span, span), span), :],
                    dqkv_all.at[:, :, head_cols], dq_ss.at[i], dq_rs.at[head], {"col": to})

    def dqkv_drain():
        @pl.when(is_head)
        def _():
            for i in range(1, n_col):
                dqkv_copy(i).wait_send()

    late.append(dqkv_drain)

    def weight_ends():
        for way in range(2):
            if n_y > 2 or way == 0:
                weight_far(y + 2 * way - 1)
            weight_step(way, 1)

    def weight_rest():
        for offset in range(2, n_y - 1):
            weight_far(y + offset)
        weight_far(y)

    def weight_both(step):
        if step < n_y:
            weight_step(0, step)
            weight_step(1, step)

    def dqkv_finish():
        for h in range(heads):
            @pl.when(c != owner(h))
            def _(h=h):
                block = dqkv_all.at[:, :, fixed_cols[h]]
                send(block, block, dq_ss.at[0], dq_rs.at[h], right).wait_recv()
        for t, ref in enumerate((dq_ref, dk_ref, dv_ref)):
            ref[0] = dqkv_all[t]

    grad_step(1)
    heads_arrive()
    forward(0, n_blocks // 2)
    grad_step(2)
    forward(n_blocks // 2, n_blocks)
    cross_start()
    ctx_start()
    cross_relay()
    cross_finish(0)
    grad_step(3)
    for copy in weight_copies:
        copy.wait()
    context_grads([0])
    grad_step(4)
    context_grads([1, 2])
    ctx_wait(0)
    grad_step(5)
    ctx_wait(1)
    ctx_in_order(middle - reach, middle + reach)
    project_ends()
    out_both(1)
    weight_near(0, n_y // 2)
    grad_step(6)
    project_middle()
    out_both(2)
    cross_finish(1)
    grad_step(7)
    near_sum()
    weight_near(n_y // 2, n_y)
    out_both(3)
    grad_step(8)
    ctx_wait(2)
    ctx_in_order(0, middle - reach)
    ctx_in_order(middle + reach, ring)
    weight_ends()
    weight_rest()
    out_both(4)
    weight_both(2)
    backward()
    weight_both(3)
    for wait in drain:
        wait()
    out_step(0, reach, final=True)
    out_step(1, reach + 1, final=True)
    for given, held in tiles:
        out_ref[0, :, given] = lo[reach, :, held].astype(BF16)
    weight_step(0, n_y, final=True)
    weight_step(1, n_y, final=True)
    dqkv_finish()
    for wait in late:
        wait()


def hand_over(*refs):
    count = len(refs) // 3
    parts, outs, held = refs[:count], refs[count:2 * count], refs[2 * count:3 * count]
    sem = refs[-1]
    inward = [pltpu.make_async_copy(parts[i], held[i], sem.at[0, i]) for i in range(count)]
    outward = [pltpu.make_async_copy(held[i], outs[i], sem.at[1, i]) for i in range(count)]
    for copy in inward:
        copy.start()
    for i in range(count):
        inward[i].wait()
        outward[i].start()
    for copy in outward:
        copy.wait()


def solution(mesh):
    n_row, n_col, n_depth = mesh.shape["row"], mesh.shape["col"], mesh.shape["depth"]

    def local(q, k, v, positions, weight, grad):
        _, span, width = q.shape
        _, rows, cols = grad.shape
        length = positions.shape[1]
        heads, ring, reach, n_y = width // HEAD_DIM, HALVES * n_row, n_row // 2, n_depth // HALVES
        stripe = cols // n_depth
        vmem = pl.BlockSpec(memory_space=pltpu.VMEM)
        anywhere = pl.BlockSpec(memory_space=pltpu.HBM)
        dma = pltpu.SemaphoreType.DMA
        hops, turns = max(reach, 1), max(n_y - 1, 1)
        scratch = [
            pltpu.VMEM((width, cols), BF16),
            pltpu.VMEM((3, span, width), BF16),
            pltpu.VMEM((3, length, HEAD_DIM), BF16),
            pltpu.VMEM((length, 128), F32),
            pltpu.VMEM((length, length), F32),
            pltpu.VMEM((length, length), BF16),
            pltpu.VMEM((length, length), BF16),
            pltpu.VMEM((length, HEAD_DIM), BF16),
            pltpu.VMEM((HALVES * length, width), BF16),
            pltpu.VMEM((HALVES * length, width), BF16),
            pltpu.VMEM((2, 2, length // 4, HEAD_DIM), BF16),
            pltpu.VMEM((ring, rows, cols), BF16),
            pltpu.VMEM((length, width), BF16),
            pltpu.VMEM((n_col, length, HEAD_DIM), BF16),
            pltpu.VMEM((length, HEAD_DIM), BF16),
            pltpu.VMEM((length, HEAD_DIM), BF16),
            pltpu.VMEM((3, length, HEAD_DIM), BF16),
            pltpu.VMEM((3, span, width), BF16),
            pltpu.VMEM((2 * reach, rows, cols), F32),
            pltpu.VMEM((hops, rows, cols), BF16),
            pltpu.VMEM((hops, rows, cols), BF16),
            pltpu.VMEM((hops, rows, cols), BF16),
            pltpu.VMEM((hops, rows, cols), BF16),
            pltpu.VMEM((n_y, 256, width), F32),
            pltpu.VMEM((2, turns, stripe // 2, width), BF16),
            pltpu.VMEM((2, turns, stripe // 2, width), BF16),
            dma((THIRDS * n_y,)), dma((THIRDS * n_y,)), dma((3,)),
            dma((heads,)), dma((n_col,)),
            dma((2, ring // 2, THIRDS)), dma((2, ring // 2, THIRDS)),
            dma((3, n_col)), dma((3, heads)), dma((2, 2, 2)), dma((2, 2, 2)),
            dma((3, heads)), dma((3, n_col)), dma((2 * reach,)), dma((n_row,)),
            dma((n_col,)), dma((heads,)),
            dma((2, hops, SUBS)), dma((2, hops, SUBS)),
            dma((2, turns)), dma((2, turns)),
        ]
        parts = pl.pallas_call(
            functools.partial(kernel, n_row, n_col, n_depth),
            out_shape=(
                jax.ShapeDtypeStruct(grad.shape, BF16),
                jax.ShapeDtypeStruct(q.shape, BF16),
                jax.ShapeDtypeStruct(k.shape, BF16),
                jax.ShapeDtypeStruct(v.shape, BF16),
                jax.ShapeDtypeStruct((stripe, width), F32),
            ),
            in_specs=[anywhere] * 3 + [vmem] + [anywhere] * 2,
            out_specs=(vmem,) * 5,
            scratch_shapes=scratch,
            compiler_params=pltpu.CompilerParams(
                collective_id=0, has_side_effects=True, vmem_limit_bytes=VMEM_BYTES
            ),
        )(q, k, v, positions, weight, grad)
        *parts, weight_grad = pl.pallas_call(
            hand_over,
            out_shape=[jax.ShapeDtypeStruct(part.shape, part.dtype) for part in parts],
            in_specs=[anywhere] * len(parts),
            out_specs=[anywhere] * len(parts),
            scratch_shapes=[pltpu.VMEM(part.shape, part.dtype) for part in parts] + [dma((2, len(parts)))],
            compiler_params=pltpu.CompilerParams(vmem_limit_bytes=VMEM_BYTES),
        )(*parts)
        return *parts, weight_grad.T

    return jax.shard_map(
        local,
        mesh=mesh,
        in_specs=(
            P("depth", "col", "row"),
            P("depth", "col", "row"),
            P("depth", "col", "row"),
            P("depth", None),
            P("row", "col"),
            P("depth", "row", "col"),
        ),
        out_specs=(
            P("depth", "row", "col"),
            P("depth", "col", "row"),
            P("depth", "col", "row"),
            P("depth", "col", "row"),
            P("row", ("col", "depth")),
        ),
        check_vma=False,
    )
```

```python
import functools

import jax
import jax.numpy as jnp
from jax import lax
from jax.experimental import pallas as pl
from jax.experimental.pallas import tpu as pltpu
from jax.sharding import PartitionSpec as P

HEAD_DIM = 128
HALVES = 2
THIRDS = 3
SUBS = 2
LANES = 128
VMEM_BYTES = 56 * 1024 * 1024
MESH = pl.DeviceIdType.MESH
F32, BF16 = jnp.float32, jnp.bfloat16

NT = (((1,), (1,)), ((), ()))
TN = (((0,), (0,)), ((), ()))


def kernel(
    n_row, n_col, n_depth,
    q_ref, k_ref, v_ref, pos_ref, w_hbm, g_ref,
    out_ref, dq_ref, dk_ref, dv_ref, dw_ref,
    w_ref, qkv_stage, qkv, pos_col, probs, probs_b, dlogits, ctx_own, ctx_all, ctx_rel, relay, grad_all,
    cg_stage, cg_recv, cg_near, cg_own, dqkv_own, dqkv_all,
    lo, rs_stage_r, rs_stage_l, rs_r, rs_l, dw_sum, dw_stage, dw_recv,
    w_sem, g_sem, in_sem, qkv_ss, qkv_rs, ag_ss, ag_rs, ctx_ss, ctx_rs, cross_ss, cross_rs, cg_ss, cg_rs, cgx_ss, cgx_rs, dq_ss, dq_rs,
    rs_ss, rs_rs, dw_ss, dw_rs,
):
    r, c, d = lax.axis_index("row"), lax.axis_index("col"), lax.axis_index("depth")
    y, b = lax.div(d, HALVES), lax.rem(d, HALVES)
    ring, n_y = HALVES * n_row, n_depth // HALVES
    reach = n_row // 2
    z = b * n_row + r
    span, width = q_ref.shape[1:]
    rows, cols = g_ref.shape[1:]
    length = pos_ref.shape[1]
    heads = width // HEAD_DIM
    scale = HEAD_DIM ** (-0.5)

    def wrap(place, size):
        place = jnp.where(place < 0, place + size, place)
        return jnp.where(place >= size, place - size, place)

    def in_half(place):
        half = jnp.where(place >= n_row, 1, 0)
        return place - half * n_row, half

    def on_ring(place):
        line, half = in_half(wrap(place, ring))
        return (line, c, y * HALVES + half)

    def on_col(place):
        return (r, place, d)

    def on_y(place):
        return (r, c, wrap(place, n_y) * HALVES + b)

    def chunk_at(offset):
        return wrap(z + offset, ring)

    def owner(h):
        return (h * n_col) // heads

    right, left, up, down = on_ring(z + 1), on_ring(z - 1), on_y(y + 1), on_y(y - 1)
    far_right, far_left, other = on_ring(z + n_row - 1), on_ring(z - n_row + 1), on_ring(z + n_row)
    middle = ring // 2
    head, is_head = 0, c == owner(0)
    for h in range(1, heads):
        head = jnp.where(c >= owner(h), h, head)
        is_head = jnp.logical_or(is_head, c == owner(h))
    head_cols = pl.ds(pl.multiple_of(head * HEAD_DIM, HEAD_DIM), HEAD_DIM)
    fixed_cols = [pl.ds(h * HEAD_DIM, HEAD_DIM) for h in range(heads)]
    sub_cols = [pl.ds(u * (cols // SUBS), cols // SUBS) for u in range(SUBS)]

    def send(src, dst, send_sem, recv_sem, to):
        return pltpu.make_async_remote_copy(
            src_ref=src, dst_ref=dst, send_sem=send_sem, recv_sem=recv_sem,
            device_id=to, device_id_type=MESH,
        )

    barrier = pltpu.get_barrier_semaphore()
    peers = [on_col(wrap(c + i, n_col)) for i in range(1, n_col)]
    peers += [right, left, other, up]
    if n_y > 2:
        peers += [down]
    if n_row > 2:
        peers += [far_right, far_left]
    for peer in peers:
        pl.semaphore_signal(barrier, inc=1, device_id=peer, device_id_type=MESH)
    third = cols // THIRDS
    tiles = [(pl.ds((n * THIRDS + t) * LANES, LANES), pl.ds(t * third + n * LANES, LANES))
             for n in range(n_y) for t in range(THIRDS)]
    weight_copies = [pltpu.make_async_copy(w_hbm.at[:, given], w_ref.at[:, held], w_sem.at[i])
                     for i, (given, held) in enumerate(tiles)]
    head_copies = [pltpu.make_async_copy(ref.at[0], qkv_stage.at[t], in_sem.at[t])
                   for t, ref in enumerate((q_ref, k_ref, v_ref))]
    grad_copies = [pltpu.make_async_copy(g_ref.at[0, :, given], grad_all.at[middle, :, held], g_sem.at[i])
                   for i, (given, held) in enumerate(tiles)]
    for copy in grad_copies + head_copies + weight_copies:
        copy.start()
    for copy in grad_copies + head_copies:
        copy.wait()
    pl.semaphore_wait(barrier, len(peers))

    drain, late = [], []

    far = [ring // 2, ring // 2 - 1]
    near = [reach, reach - 1]
    third_cols = [pl.ds(u * third, third) for u in range(THIRDS)]

    def grad_copy(way, step, u):
        sign = -1 if way == 0 else 1
        return send(grad_all.at[middle + sign * (step - 1), :, third_cols[u]],
                    grad_all.at[middle + sign * step, :, third_cols[u]],
                    ag_ss.at[way, step - 1, u], ag_rs.at[way, step - 1, u], right if way == 0 else left)

    def where_needed(place, way, step, u, action):
        if step <= near[way] or u == 1:
            action()
            return
        line, half = in_half(wrap(place, ring))
        onward = far[way] - step
        crosses = line + onward >= n_row if way == 0 else line - onward < 0
        pl.when(jnp.logical_or(crosses, half == (0 if u == 0 else 1)))(action)

    def grad_start(way, step, u):
        where_needed(z + (1 if way == 0 else -1), way, step, u, grad_copy(way, step, u).start)

    def grad_step(step):
        for u in (1, 0, 2):
            for way in range(2):
                if step <= far[way]:
                    def pass_on(way=way, u=u):
                        grad_copy(way, step, u).wait_recv()
                        if step < far[way]:
                            grad_start(way, step + 1, u)

                    where_needed(z, way, step, u, pass_on)

    def grad_drain():
        for way in range(2):
            for step in range(1, far[way] + 1):
                for u in range(THIRDS):
                    where_needed(z + (1 if way == 0 else -1), way, step, u, grad_copy(way, step, u).wait_send)

    drain.append(grad_drain)
    for u in (1, 0, 2):
        for way in range(2):
            grad_start(way, 1, u)

    own_span = pl.ds(pl.multiple_of(c * span, span), span)
    def heads_copy(h):
        return send(qkv_stage.at[:, :, fixed_cols[h]], qkv.at[:, own_span, :],
                    qkv_ss.at[h], qkv_rs.at[c], on_col(owner(h)))

    for h in range(heads):
        @pl.when(c != owner(h))
        def _(h=h):
            heads_copy(h).start()

    @pl.when(is_head)
    def _():
        for t in range(3):
            qkv[t, own_span, :] = qkv_stage[t, :, head_cols]

    def heads_drain():
        for h in range(heads):
            @pl.when(c != owner(h))
            def _(h=h):
                heads_copy(h).wait_send()

    drain.append(heads_drain)

    block_rows = min(128, length)

    def forward(phase):
        @pl.when(is_head)
        def _():
            base = crossing_half(r, phase) * half_rows
            for i in range(n_blocks // 2):
                at = pl.ds(pl.multiple_of(base + i * block_rows, block_rows), block_rows)
                logits = lax.dot_general(qkv[0, at, :], qkv[1], NT, preferred_element_type=F32)
                visible = pos_ref[...].astype(F32) <= pos_col[at, 0:1]
                logits = jnp.where(visible, logits * scale, -jnp.inf)
                highest = jnp.max(logits, axis=-1, keepdims=True)
                grown = jnp.exp(logits - highest)
                prob = grown * (1.0 / jnp.sum(grown, axis=-1, keepdims=True))
                probs[at, :] = prob
                rounded = prob.astype(BF16)
                probs_b[at, :] = rounded
                context = jnp.dot(rounded, qkv[2], preferred_element_type=F32)
                ctx_own[at, :] = context.astype(BF16)

    n_blocks = length // block_rows

    def heads_arrive():
        @pl.when(is_head)
        def _():
            pos_col[...] = jnp.transpose(
                jnp.broadcast_to(pos_ref[...].astype(F32), (128, length))
            )
            for i in range(1, n_col):
                src = wrap(c + i, n_col)
                place = qkv.at[:, pl.ds(pl.multiple_of(src * span, span), span), :]
                send(place, place, qkv_ss.at[0], qkv_rs.at[src], on_col(src)).wait_recv()

    half_rows, quarter = length // 2, length // 4

    def ctx_rows(group):
        if group == 0:
            return pl.ds(pl.multiple_of(b * length, length), length)
        return crossing_rows(1 - b, r, group - 1)

    def crossing_half(line, phase):
        return jnp.where(line < reach, 1 - phase, phase)

    def crossing_rows(place, line, phase):
        start = place * length + crossing_half(line, phase) * half_rows
        return pl.ds(pl.multiple_of(start, half_rows), half_rows)

    def crossing_part(place, line, phase, way):
        start = place * length + crossing_half(line, phase) * half_rows + way * quarter
        return pl.ds(pl.multiple_of(start, quarter), quarter)

    def cross_copy(phase, way):
        return send(ctx_own.at[crossing_part(0, r, phase, way), :], relay.at[phase, way],
                    cross_ss.at[0, phase, way], cross_rs.at[0, phase, way], right if way == 0 else left)

    def relay_copy(phase, way):
        origin = chunk_at(-1 if way == 0 else 1)
        line, half = in_half(origin)
        at = crossing_part(half, line, phase, way)
        return send(relay.at[phase, way], ctx_all.at[at, head_cols],
                    cross_ss.at[1, phase, way], cross_rs.at[1, phase, way], far_right if way == 0 else far_left)

    def cross_arrives(phase, way):
        block = ctx_all.at[crossing_part(1 - b, r, phase, way), head_cols]
        send(block, block, cross_ss.at[1, phase, way], cross_rs.at[1, phase, way], far_right).wait_recv()

    def ctx_copies(group):
        src = ctx_own if group == 0 else ctx_all.at[ctx_rows(group), head_cols]
        targets = [on_col(wrap(c + i, n_col)) for i in range(1, n_col)]
        return [
            send(src, ctx_all.at[ctx_rows(group), head_cols], ctx_ss.at[group, i], ctx_rs.at[group, head], to)
            for i, to in enumerate(targets)
        ]

    def ctx_block(half, h):
        block = ctx_all.at[ctx_rows(half), fixed_cols[h]]
        return send(block, block, ctx_ss.at[0, 0], ctx_rs.at[half, h], right)

    def ctx_wait(half):
        for h in range(heads):
            @pl.when(c != owner(h))
            def _(h=h):
                ctx_block(half, h).wait_recv()

    def cross_start(phase):
        @pl.when(is_head)
        def _():
            for way in range(2):
                cross_copy(phase, way).start()

    def ctx_start():
        @pl.when(is_head)
        def _():
            for copy in ctx_copies(0):
                copy.start()
            ctx_all[ctx_rows(0), head_cols] = ctx_own[...]

    def cross_relay(phase):
        @pl.when(is_head)
        def _():
            for way in range(2):
                cross_copy(phase, way).wait_recv()
                relay_copy(phase, way).start()

    def cross_finish(phase):
        @pl.when(is_head)
        def _():
            for way in range(2):
                cross_arrives(phase, way)
            for copy in ctx_copies(1 + phase):
                copy.start()

    def ctx_in_order(first, last):
        for slot in range(first, last):
            held = chunk_at(slot - middle)
            ctx_rel[slot * rows:(slot + 1) * rows, :] = ctx_all[pl.ds(pl.multiple_of(held * rows, rows), rows), :]

    def ctx_drain():
        @pl.when(is_head)
        def _():
            for phase in range(2):
                for way in range(2):
                    cross_copy(phase, way).wait_send()
                    relay_copy(phase, way).wait_send()
            for group in range(3):
                for copy in ctx_copies(group):
                    copy.wait_send()
    drain.append(ctx_drain)

    inner = reach // 2
    near_slots = [list(range(reach - inner, reach + inner)),
                  list(range(reach - inner)) + list(range(reach + inner, 2 * reach))]
    held_at = {slot: i for i, slot in enumerate(near_slots[0] + near_slots[1])}
    near_parts = [(0, 2 * inner), (2 * inner, 2 * reach - 2 * inner)]

    def near_copy(part, h):
        at = pl.ds(near_parts[part][0] * rows, near_parts[part][1] * rows)
        return send(cg_stage.at[at, fixed_cols[h]], cg_recv.at[c, at, :],
                    cg_ss.at[part, h], cg_rs.at[part, c], on_col(owner(h)))

    def context_grads(part):
        first, count = near_parts[part]
        if count == 0:
            return
        tokens = jnp.concatenate([grad_all[middle - reach + slot] for slot in near_slots[part]], axis=0)
        for i in range(heads // 2):
            two = pl.ds(i * 2 * HEAD_DIM, 2 * HEAD_DIM)
            product = lax.dot_general(tokens, w_ref[two, :], NT, preferred_element_type=F32)
            cg_stage[first * rows:(first + count) * rows, two] = product.astype(BF16)
            for h in (2 * i, 2 * i + 1):
                @pl.when(c != owner(h))
                def _(h=h):
                    near_copy(part, h).start()

    def near_sum():
        @pl.when(is_head)
        def _():
            cg_recv[c] = cg_stage[:, head_cols]
            for i in range(1, n_col):
                src = wrap(c + i, n_col)
                for part, (first, count) in enumerate(near_parts):
                    if count > 0:
                        block = cg_recv.at[src, pl.ds(first * rows, count * rows), :]
                        send(block, block, cg_ss.at[part, 0], cg_rs.at[part, src], on_col(src)).wait_recv()
            for i in range(2 * reach):
                at = pl.ds(i * rows, rows)
                total = cg_recv[0, at, :].astype(F32)
                for k in range(1, n_col):
                    total = total + cg_recv[k, at, :].astype(F32)
                cg_near[at, :] = total.astype(BF16)
            for i in range(2 * reach):
                @pl.when(is_own(i))
                def _(i=i):
                    cg_own[near_rows(i), :] = cg_near[held_at[i] * rows:(held_at[i] + 1) * rows, :]

                @pl.when(jnp.logical_not(is_own(i)))
                def _(i=i):
                    near_cross(i).start()

    def is_own(i):
        block = r + i - reach
        return jnp.logical_and(block >= 0, block < n_row)

    def near_block(i):
        return wrap(r + i - reach, n_row)

    def near_rows(i):
        return pl.ds(pl.multiple_of(near_block(i) * rows, rows), rows)

    def near_cross(i):
        return send(cg_near.at[pl.ds(held_at[i] * rows, rows), :], cg_own.at[near_rows(i), :],
                    cgx_ss.at[i], cgx_rs.at[near_block(i)], other)

    def cross_wait():
        for block in range(n_row):
            offset = block - r

            @pl.when(jnp.logical_or(offset < -reach, offset >= reach))
            def _(block=block):
                at = cg_own.at[pl.ds(block * rows, rows), :]
                send(at, at, cgx_ss.at[0], cgx_rs.at[block], other).wait_recv()

    def cg_drain():
        for part, (_, count) in enumerate(near_parts):
            if count > 0:
                for h in range(heads):
                    @pl.when(c != owner(h))
                    def _(part=part, h=h):
                        near_copy(part, h).wait_send()
        for i in range(2 * reach):
            @pl.when(jnp.logical_and(is_head, jnp.logical_not(is_own(i))))
            def _(i=i):
                near_cross(i).wait_send()

    drain.append(cg_drain)

    tile = cols // 3

    def project(first, last):
        tokens = ctx_rel[(middle - reach + first) * rows:(middle - reach + last) * rows, :]

        @pl.loop(0, 3)
        def _(i):
            at = pl.ds(pl.multiple_of(i * tile, tile), tile)
            product = jnp.dot(tokens, w_ref[:, at], preferred_element_type=F32)
            lo[first:last, :, at] = product.reshape(last - first, rows, tile)

    def project_ends():
        project(0, 2)
        if reach > 1:
            project(2 * reach - 2, 2 * reach)

    def project_middle():
        if reach > 2:
            project(2, 2 * reach - 2)

    def out_step(way, step, final=False):
        stage, landed = (rs_stage_r, rs_r) if way == 0 else (rs_stage_l, rs_l)
        place = (2 * reach - step) if way == 0 else step - 1
        for u in range(SUBS):
            total = lo[place, :, sub_cols[u]]
            if step > 1:
                block = landed.at[step - 2, :, sub_cols[u]]
                send(block, block, rs_ss.at[way, step - 2, u], rs_rs.at[way, step - 2, u], right).wait_recv()
                total = total + block[...].astype(F32)
            if final:
                lo[place, :, sub_cols[u]] = total
                continue
            stage[step - 1, :, sub_cols[u]] = total.astype(BF16)
            copy = send(stage.at[step - 1, :, sub_cols[u]], landed.at[step - 1, :, sub_cols[u]],
                        rs_ss.at[way, step - 1, u], rs_rs.at[way, step - 1, u], right if way == 0 else left)
            copy.start()
            (drain if step < 3 else late).append(copy.wait_send)

    def out_both(step):
        if step < reach:
            out_step(0, step)
        if step <= reach:
            out_step(1, step)

    stripe = cols // n_depth
    part = stripe // 2

    def weight_product(place, first, last):
        pair = [
            grad_all[first:last, :, pl.ds(pl.multiple_of((b + i) * third + place * LANES, LANES), LANES)]
            for i in range(2)
        ]
        tokens = jnp.concatenate(pair, axis=-1).reshape((last - first) * rows, 2 * LANES)
        return lax.dot_general(tokens, ctx_rel[first * rows:last * rows, :], TN, preferred_element_type=F32)

    def weight_near(first, last):
        @pl.loop(first, last)
        def _(place):
            dw_sum[place] = weight_product(place, middle - reach, middle + reach)

    def weight_far(place):
        place = wrap(place, n_y)
        dw_sum[place] += weight_product(place, 0, middle - reach) + weight_product(place, middle + reach, ring)

    def weight_step(way, step, final=False):
        place = wrap(wrap(y + (-step if way == 0 else step), n_y), n_y)
        own = slice(way * part, (way + 1) * part)
        total = dw_sum[place, pl.ds(pl.multiple_of(b * 64 + way * part, 32), part), :]
        if step > 1:
            block = dw_recv.at[way, step - 2]
            send(block, block, dw_ss.at[way, step - 2], dw_rs.at[way, step - 2], up).wait_recv()
            total = total + block[...].astype(F32)
        if final:
            dw_ref[own, :] = total
            return
        dw_stage[way, step - 1] = total.astype(BF16)
        copy = send(dw_stage.at[way, step - 1], dw_recv.at[way, step - 1], dw_ss.at[way, step - 1],
                    dw_rs.at[way, step - 1], up if way == 0 else down)
        copy.start()
        late.append(copy.wait_send)

    def backward():
        @pl.when(is_head)
        def _():
            cross_wait()
            for i in range(n_blocks):
                at = pl.ds(i * block_rows, block_rows)
                grad = cg_own[at, :]
                row_dot = jnp.sum(grad.astype(F32) * ctx_own[at, :].astype(F32), axis=-1, keepdims=True)
                dprob = lax.dot_general(grad, qkv[2], NT, preferred_element_type=F32)
                rounded = (probs[at, :] * (dprob - row_dot)).astype(BF16)
                dlogits[at, :] = rounded
                query_grad = jnp.dot(rounded, qkv[1], preferred_element_type=F32) * scale
                dqkv_own[0, at, :] = query_grad.astype(BF16)
            key_grad = lax.dot_general(dlogits[...], qkv[0], TN, preferred_element_type=F32) * scale
            dqkv_own[1] = key_grad.astype(BF16)
            value_grad = lax.dot_general(probs_b[...], cg_own[...], TN, preferred_element_type=F32)
            dqkv_own[2] = value_grad.astype(BF16)
            for i in range(1, n_col):
                dqkv_copy(i).start()
            for t in range(3):
                dqkv_all[t, :, head_cols] = dqkv_own[t, own_span, :]

    def dqkv_copy(i):
        to = wrap(c + i, n_col)
        return send(dqkv_own.at[:, pl.ds(pl.multiple_of(to * span, span), span), :],
                    dqkv_all.at[:, :, head_cols], dq_ss.at[i], dq_rs.at[head], on_col(to))

    def dqkv_drain():
        @pl.when(is_head)
        def _():
            for i in range(1, n_col):
                dqkv_copy(i).wait_send()

    late.append(dqkv_drain)

    def weight_ends():
        for way in range(2):
            if n_y > 2 or way == 0:
                weight_far(y + 2 * way - 1)
            weight_step(way, 1)

    def weight_rest():
        for offset in range(2, n_y - 1):
            weight_far(y + offset)
        weight_far(y)

    def weight_both(step):
        if step < n_y:
            weight_step(0, step)
            weight_step(1, step)

    def dqkv_finish():
        for h in range(heads):
            @pl.when(c != owner(h))
            def _(h=h):
                block = dqkv_all.at[:, :, fixed_cols[h]]
                send(block, block, dq_ss.at[0], dq_rs.at[h], right).wait_recv()
        for t, ref in enumerate((dq_ref, dk_ref, dv_ref)):
            ref[0] = dqkv_all[t]

    grad_step(1)
    heads_arrive()
    forward(0)
    cross_start(0)
    grad_step(2)
    forward(1)
    cross_relay(0)
    cross_start(1)
    ctx_start()
    cross_relay(1)
    cross_finish(0)
    grad_step(3)
    for copy in weight_copies:
        copy.wait()
    context_grads(0)
    grad_step(4)
    context_grads(1)
    ctx_wait(0)
    grad_step(5)
    ctx_wait(1)
    ctx_in_order(middle - reach, middle + reach)
    project_ends()
    out_both(1)
    weight_near(0, n_y // 2)
    grad_step(6)
    project_middle()
    out_both(2)
    cross_finish(1)
    grad_step(7)
    near_sum()
    weight_near(n_y // 2, n_y)
    out_both(3)
    grad_step(8)
    ctx_wait(2)
    ctx_in_order(0, middle - reach)
    ctx_in_order(middle + reach, ring)
    weight_ends()
    weight_rest()
    out_both(4)
    weight_both(2)
    backward()
    weight_both(3)
    for wait in drain:
        wait()
    out_step(0, reach, final=True)
    out_step(1, reach + 1, final=True)
    for given, held in tiles:
        out_ref[0, :, given] = lo[reach, :, held].astype(BF16)
    weight_step(0, n_y, final=True)
    weight_step(1, n_y, final=True)
    dqkv_finish()
    for wait in late:
        wait()


def hand_over(*refs):
    count = len(refs) // 3
    parts, outs, held = refs[:count], refs[count:2 * count], refs[2 * count:3 * count]
    sem = refs[-1]
    inward = [pltpu.make_async_copy(parts[i], held[i], sem.at[0, i]) for i in range(count)]
    outward = [pltpu.make_async_copy(held[i], outs[i], sem.at[1, i]) for i in range(count)]
    for copy in inward:
        copy.start()
    for i in range(count):
        inward[i].wait()
        outward[i].start()
    for copy in outward:
        copy.wait()


def solution(mesh):
    n_row, n_col, n_depth = mesh.shape["row"], mesh.shape["col"], mesh.shape["depth"]

    def local(q, k, v, positions, weight, grad):
        _, span, width = q.shape
        _, rows, cols = grad.shape
        length = positions.shape[1]
        heads, ring, reach, n_y = width // HEAD_DIM, HALVES * n_row, n_row // 2, n_depth // HALVES
        stripe = cols // n_depth
        vmem = pl.BlockSpec(memory_space=pltpu.VMEM)
        anywhere = pl.BlockSpec(memory_space=pltpu.HBM)
        dma = pltpu.SemaphoreType.DMA
        hops, turns = max(reach, 1), max(n_y - 1, 1)
        scratch = [
            pltpu.VMEM((width, cols), BF16),
            pltpu.VMEM((3, span, width), BF16),
            pltpu.VMEM((3, length, HEAD_DIM), BF16),
            pltpu.VMEM((length, 128), F32),
            pltpu.VMEM((length, length), F32),
            pltpu.VMEM((length, length), BF16),
            pltpu.VMEM((length, length), BF16),
            pltpu.VMEM((length, HEAD_DIM), BF16),
            pltpu.VMEM((HALVES * length, width), BF16),
            pltpu.VMEM((HALVES * length, width), BF16),
            pltpu.VMEM((2, 2, length // 4, HEAD_DIM), BF16),
            pltpu.VMEM((ring, rows, cols), BF16),
            pltpu.VMEM((length, width), BF16),
            pltpu.VMEM((n_col, length, HEAD_DIM), BF16),
            pltpu.VMEM((length, HEAD_DIM), BF16),
            pltpu.VMEM((length, HEAD_DIM), BF16),
            pltpu.VMEM((3, length, HEAD_DIM), BF16),
            pltpu.VMEM((3, span, width), BF16),
            pltpu.VMEM((2 * reach, rows, cols), F32),
            pltpu.VMEM((hops, rows, cols), BF16),
            pltpu.VMEM((hops, rows, cols), BF16),
            pltpu.VMEM((hops, rows, cols), BF16),
            pltpu.VMEM((hops, rows, cols), BF16),
            pltpu.VMEM((n_y, 256, width), F32),
            pltpu.VMEM((2, turns, stripe // 2, width), BF16),
            pltpu.VMEM((2, turns, stripe // 2, width), BF16),
            dma((THIRDS * n_y,)), dma((THIRDS * n_y,)), dma((3,)),
            dma((heads,)), dma((n_col,)),
            dma((2, ring // 2, THIRDS)), dma((2, ring // 2, THIRDS)),
            dma((3, n_col)), dma((3, heads)), dma((2, 2, 2)), dma((2, 2, 2)),
            dma((2, heads)), dma((2, n_col)), dma((2 * reach,)), dma((n_row,)),
            dma((n_col,)), dma((heads,)),
            dma((2, hops, SUBS)), dma((2, hops, SUBS)),
            dma((2, turns)), dma((2, turns)),
        ]
        parts = pl.pallas_call(
            functools.partial(kernel, n_row, n_col, n_depth),
            out_shape=(
                jax.ShapeDtypeStruct(grad.shape, BF16),
                jax.ShapeDtypeStruct(q.shape, BF16),
                jax.ShapeDtypeStruct(k.shape, BF16),
                jax.ShapeDtypeStruct(v.shape, BF16),
                jax.ShapeDtypeStruct((stripe, width), F32),
            ),
            in_specs=[anywhere] * 3 + [vmem] + [anywhere] * 2,
            out_specs=(vmem,) * 5,
            scratch_shapes=scratch,
            compiler_params=pltpu.CompilerParams(
                collective_id=0, has_side_effects=True, vmem_limit_bytes=VMEM_BYTES
            ),
        )(q, k, v, positions, weight, grad)
        *parts, weight_grad = pl.pallas_call(
            hand_over,
            out_shape=[jax.ShapeDtypeStruct(part.shape, part.dtype) for part in parts],
            in_specs=[anywhere] * len(parts),
            out_specs=[anywhere] * len(parts),
            scratch_shapes=[pltpu.VMEM(part.shape, part.dtype) for part in parts] + [dma((2, len(parts)))],
            compiler_params=pltpu.CompilerParams(vmem_limit_bytes=VMEM_BYTES),
        )(*parts)
        return *parts, weight_grad.T

    return jax.shard_map(
        local,
        mesh=mesh,
        in_specs=(
            P("depth", "col", "row"),
            P("depth", "col", "row"),
            P("depth", "col", "row"),
            P("depth", None),
            P("row", "col"),
            P("depth", "row", "col"),
        ),
        out_specs=(
            P("depth", "row", "col"),
            P("depth", "col", "row"),
            P("depth", "col", "row"),
            P("depth", "col", "row"),
            P("row", ("col", "depth")),
        ),
        check_vma=False,
    )
```

```python
import functools

import jax
import jax.numpy as jnp
from jax import lax
from jax.experimental import pallas as pl
from jax.experimental.pallas import tpu as pltpu
from jax.sharding import PartitionSpec as P

HEAD_DIM = 128
HALVES = 2
PARTS = 2
SUBS = 2
LANES = 128
VMEM_BYTES = 56 * 1024 * 1024
MESH = pl.DeviceIdType.MESH
F32, BF16 = jnp.float32, jnp.bfloat16

NT = (((1,), (1,)), ((), ()))
TN = (((0,), (0,)), ((), ()))


def kernel(
    n_row, n_col, n_depth,
    q_ref, k_ref, v_ref, pos_ref, w_hbm, g_ref,
    out_ref, dq_ref, dk_ref, dv_ref, dw_ref,
    w_ref, w_mid, g_mid, qkv_stage, qkv, pos_col, probs, probs_b, dlogits, ctx_own, ctx_all, ctx_rel, relay, grad_all,
    cg_stage, cg_recv, cg_near, cg_own, dqkv_own, dqkv_all,
    lo, rs_stage_r, rs_stage_l, rs_r, rs_l, dw_sum, dw_stage, dw_recv,
    w_sem, g_sem, in_sem, qkv_ss, qkv_rs, ag_ss, ag_rs, ctx_ss, ctx_rs, cross_ss, cross_rs, cg_ss, cg_rs, cgx_ss, cgx_rs, dq_ss, dq_rs,
    rs_ss, rs_rs, dw_ss, dw_rs,
):
    r, c, d = lax.axis_index("row"), lax.axis_index("col"), lax.axis_index("depth")
    y, b = lax.div(d, HALVES), lax.rem(d, HALVES)
    ring, n_y = HALVES * n_row, n_depth // HALVES
    reach = n_row // 2
    z = b * n_row + r
    span, width = q_ref.shape[1:]
    rows, cols = g_ref.shape[1:]
    length = pos_ref.shape[1]
    heads = width // HEAD_DIM
    scale = HEAD_DIM ** (-0.5)

    def wrap(place, size):
        place = jnp.where(place < 0, place + size, place)
        return jnp.where(place >= size, place - size, place)

    def in_half(place):
        half = jnp.where(place >= n_row, 1, 0)
        return place - half * n_row, half

    def on_ring(place):
        line, half = in_half(wrap(place, ring))
        return (line, c, y * HALVES + half)

    def on_col(place):
        return (r, place, d)

    def on_y(place):
        return (r, c, wrap(place, n_y) * HALVES + b)

    def chunk_at(offset):
        return wrap(z + offset, ring)

    def owner(h):
        return (h * n_col) // heads

    right, left, up, down = on_ring(z + 1), on_ring(z - 1), on_y(y + 1), on_y(y - 1)
    far_right, far_left, other = on_ring(z + n_row - 1), on_ring(z - n_row + 1), on_ring(z + n_row)
    middle = ring // 2
    head, is_head = 0, c == owner(0)
    for h in range(1, heads):
        head = jnp.where(c >= owner(h), h, head)
        is_head = jnp.logical_or(is_head, c == owner(h))
    head_cols = pl.ds(pl.multiple_of(head * HEAD_DIM, HEAD_DIM), HEAD_DIM)
    fixed_cols = [pl.ds(h * HEAD_DIM, HEAD_DIM) for h in range(heads)]
    sub_cols = [pl.ds(u * (cols // SUBS), cols // SUBS) for u in range(SUBS)]

    def send(src, dst, send_sem, recv_sem, to):
        return pltpu.make_async_remote_copy(
            src_ref=src, dst_ref=dst, send_sem=send_sem, recv_sem=recv_sem,
            device_id=to, device_id_type=MESH,
        )

    barrier = pltpu.get_barrier_semaphore()
    peers = [on_col(wrap(c + i, n_col)) for i in range(1, n_col)]
    peers += [right, left, other, up]
    if n_y > 2:
        peers += [down]
    if n_row > 2:
        peers += [far_right, far_left]
    for peer in peers:
        pl.semaphore_signal(barrier, inc=1, device_id=peer, device_id_type=MESH)
    part_cols = cols // PARTS
    lines = n_y * LANES
    whole = [(pl.ds((n * 3 + 2 * u) * LANES, LANES), pl.ds(u * part_cols + n * LANES, LANES))
             for n in range(n_y) for u in range(PARTS)]
    middles = [pl.ds((n * 3 + 1) * LANES, LANES) for n in range(n_y)]

    def middle_at(u, n):
        return pl.ds(u * part_cols + lines + (n // 2) * LANES, LANES)

    def swap_middles(first, second):
        lower = lax.broadcasted_iota(jnp.int32, first.shape, 1) < LANES // 2
        return (jnp.where(lower, first, pltpu.roll(second, LANES // 2, 1)),
                jnp.where(lower, pltpu.roll(first, LANES // 2, 1), second))

    def place_middles(staged, held):
        for n in range(0, n_y, 2):
            pair = [staged[:, (n + i) * LANES:(n + i + 1) * LANES].astype(F32) for i in range(2)]
            for u, tile_values in enumerate(swap_middles(*pair)):
                held[:, middle_at(u, n)] = tile_values.astype(BF16)

    weight_copies = [pltpu.make_async_copy(w_hbm.at[:, given], w_ref.at[:, held], w_sem.at[i])
                     for i, (given, held) in enumerate(whole)]
    weight_copies += [pltpu.make_async_copy(w_hbm.at[:, given], w_mid.at[:, pl.ds(n * LANES, LANES)], w_sem.at[2 * n_y + n])
                      for n, given in enumerate(middles)]
    head_copies = [pltpu.make_async_copy(ref.at[0], qkv_stage.at[t], in_sem.at[t])
                   for t, ref in enumerate((q_ref, k_ref, v_ref))]
    grad_copies = [pltpu.make_async_copy(g_ref.at[0, :, given], grad_all.at[middle, :, held], g_sem.at[i])
                   for i, (given, held) in enumerate(whole)]
    grad_copies += [pltpu.make_async_copy(g_ref.at[0, :, given], g_mid.at[:, pl.ds(n * LANES, LANES)], g_sem.at[2 * n_y + n])
                    for n, given in enumerate(middles)]
    for copy in grad_copies + head_copies + weight_copies:
        copy.start()
    for copy in grad_copies + head_copies:
        copy.wait()
    place_middles(g_mid, grad_all.at[middle])
    pl.semaphore_wait(barrier, len(peers))

    drain, late = [], []

    far = [ring // 2, ring // 2 - 1]
    near = [reach, reach - 1]
    held_cols = [pl.ds(u * part_cols, part_cols) for u in range(PARTS)]

    def grad_copy(way, step, u):
        sign = -1 if way == 0 else 1
        return send(grad_all.at[middle + sign * (step - 1), :, held_cols[u]],
                    grad_all.at[middle + sign * step, :, held_cols[u]],
                    ag_ss.at[way, step - 1, u], ag_rs.at[way, step - 1, u], right if way == 0 else left)

    def where_needed(place, way, step, u, action):
        if step <= near[way]:
            action()
            return
        line, half = in_half(wrap(place, ring))
        onward = far[way] - step
        crosses = line + onward >= n_row if way == 0 else line - onward < 0
        pl.when(jnp.logical_or(crosses, half == u))(action)

    def grad_start(way, step, u):
        where_needed(z + (1 if way == 0 else -1), way, step, u, grad_copy(way, step, u).start)

    def grad_step(step):
        for u in range(PARTS):
            for way in range(2):
                if step <= far[way]:
                    def pass_on(way=way, u=u):
                        grad_copy(way, step, u).wait_recv()
                        if step < far[way]:
                            grad_start(way, step + 1, u)

                    where_needed(z, way, step, u, pass_on)

    def grad_drain():
        for way in range(2):
            for step in range(1, far[way] + 1):
                for u in range(PARTS):
                    where_needed(z + (1 if way == 0 else -1), way, step, u, grad_copy(way, step, u).wait_send)

    drain.append(grad_drain)
    for u in range(PARTS):
        for way in range(2):
            grad_start(way, 1, u)

    own_span = pl.ds(pl.multiple_of(c * span, span), span)
    def heads_copy(h):
        return send(qkv_stage.at[:, :, fixed_cols[h]], qkv.at[:, own_span, :],
                    qkv_ss.at[h], qkv_rs.at[c], on_col(owner(h)))

    for h in range(heads):
        @pl.when(c != owner(h))
        def _(h=h):
            heads_copy(h).start()

    @pl.when(is_head)
    def _():
        for t in range(3):
            qkv[t, own_span, :] = qkv_stage[t, :, head_cols]

    def heads_drain():
        for h in range(heads):
            @pl.when(c != owner(h))
            def _(h=h):
                heads_copy(h).wait_send()

    drain.append(heads_drain)

    block_rows = min(128, length)

    def forward(phase):
        @pl.when(is_head)
        def _():
            base = crossing_half(r, phase) * half_rows
            for i in range(n_blocks // 2):
                at = pl.ds(pl.multiple_of(base + i * block_rows, block_rows), block_rows)
                logits = lax.dot_general(qkv[0, at, :], qkv[1], NT, preferred_element_type=F32)
                visible = pos_ref[...].astype(F32) <= pos_col[at, 0:1]
                logits = jnp.where(visible, logits * scale, -jnp.inf)
                highest = jnp.max(logits, axis=-1, keepdims=True)
                grown = jnp.exp(logits - highest)
                prob = grown * (1.0 / jnp.sum(grown, axis=-1, keepdims=True))
                probs[at, :] = prob
                rounded = prob.astype(BF16)
                probs_b[at, :] = rounded
                context = jnp.dot(rounded, qkv[2], preferred_element_type=F32)
                ctx_own[at, :] = context.astype(BF16)

    n_blocks = length // block_rows

    def heads_arrive():
        @pl.when(is_head)
        def _():
            pos_col[...] = jnp.transpose(
                jnp.broadcast_to(pos_ref[...].astype(F32), (128, length))
            )
            for i in range(1, n_col):
                src = wrap(c + i, n_col)
                place = qkv.at[:, pl.ds(pl.multiple_of(src * span, span), span), :]
                send(place, place, qkv_ss.at[0], qkv_rs.at[src], on_col(src)).wait_recv()

    half_rows, quarter = length // 2, length // 4

    def ctx_rows(group):
        if group == 0:
            return pl.ds(pl.multiple_of(b * length, length), length)
        return crossing_rows(1 - b, r, group - 1)

    def crossing_half(line, phase):
        return jnp.where(line < reach, 1 - phase, phase)

    def crossing_rows(place, line, phase):
        start = place * length + crossing_half(line, phase) * half_rows
        return pl.ds(pl.multiple_of(start, half_rows), half_rows)

    def crossing_part(place, line, phase, way):
        start = place * length + crossing_half(line, phase) * half_rows + way * quarter
        return pl.ds(pl.multiple_of(start, quarter), quarter)

    def cross_copy(phase, way):
        return send(ctx_own.at[crossing_part(0, r, phase, way), :], relay.at[phase, way],
                    cross_ss.at[0, phase, way], cross_rs.at[0, phase, way], right if way == 0 else left)

    def relay_copy(phase, way):
        origin = chunk_at(-1 if way == 0 else 1)
        line, half = in_half(origin)
        at = crossing_part(half, line, phase, way)
        return send(relay.at[phase, way], ctx_all.at[at, head_cols],
                    cross_ss.at[1, phase, way], cross_rs.at[1, phase, way], far_right if way == 0 else far_left)

    def cross_arrives(phase, way):
        block = ctx_all.at[crossing_part(1 - b, r, phase, way), head_cols]
        send(block, block, cross_ss.at[1, phase, way], cross_rs.at[1, phase, way], far_right).wait_recv()

    def ctx_copies(group):
        src = ctx_own if group == 0 else ctx_all.at[ctx_rows(group), head_cols]
        targets = [on_col(wrap(c + i, n_col)) for i in range(1, n_col)]
        return [
            send(src, ctx_all.at[ctx_rows(group), head_cols], ctx_ss.at[group, i], ctx_rs.at[group, head], to)
            for i, to in enumerate(targets)
        ]

    def ctx_block(half, h):
        block = ctx_all.at[ctx_rows(half), fixed_cols[h]]
        return send(block, block, ctx_ss.at[0, 0], ctx_rs.at[half, h], right)

    def ctx_wait(half):
        for h in range(heads):
            @pl.when(c != owner(h))
            def _(h=h):
                ctx_block(half, h).wait_recv()

    def cross_start(phase):
        @pl.when(is_head)
        def _():
            for way in range(2):
                cross_copy(phase, way).start()

    def ctx_start():
        @pl.when(is_head)
        def _():
            for copy in ctx_copies(0):
                copy.start()
            ctx_all[ctx_rows(0), head_cols] = ctx_own[...]

    def cross_relay(phase):
        @pl.when(is_head)
        def _():
            for way in range(2):
                cross_copy(phase, way).wait_recv()
                relay_copy(phase, way).start()

    def cross_finish(phase):
        @pl.when(is_head)
        def _():
            for way in range(2):
                cross_arrives(phase, way)
            for copy in ctx_copies(1 + phase):
                copy.start()

    def ctx_in_order(first, last):
        for slot in range(first, last):
            held = chunk_at(slot - middle)
            ctx_rel[slot * rows:(slot + 1) * rows, :] = ctx_all[pl.ds(pl.multiple_of(held * rows, rows), rows), :]

    def ctx_drain():
        @pl.when(is_head)
        def _():
            for phase in range(2):
                for way in range(2):
                    cross_copy(phase, way).wait_send()
                    relay_copy(phase, way).wait_send()
            for group in range(3):
                for copy in ctx_copies(group):
                    copy.wait_send()
    drain.append(ctx_drain)

    inner = reach // 2
    near_slots = [list(range(reach - inner, reach + inner)),
                  list(range(reach - inner)) + list(range(reach + inner, 2 * reach))]
    held_at = {slot: i for i, slot in enumerate(near_slots[0] + near_slots[1])}
    near_parts = [(0, 2 * inner), (2 * inner, 2 * reach - 2 * inner)]

    def near_copy(part, h):
        at = pl.ds(near_parts[part][0] * rows, near_parts[part][1] * rows)
        return send(cg_stage.at[at, fixed_cols[h]], cg_recv.at[c, at, :],
                    cg_ss.at[part, h], cg_rs.at[part, c], on_col(owner(h)))

    def context_grads(part):
        first, count = near_parts[part]
        if count == 0:
            return
        tokens = jnp.concatenate([grad_all[middle - reach + slot] for slot in near_slots[part]], axis=0)
        for i in range(heads // 2):
            two = pl.ds(i * 2 * HEAD_DIM, 2 * HEAD_DIM)
            product = lax.dot_general(tokens, w_ref[two, :], NT, preferred_element_type=F32)
            cg_stage[first * rows:(first + count) * rows, two] = product.astype(BF16)
            for h in (2 * i, 2 * i + 1):
                @pl.when(c != owner(h))
                def _(h=h):
                    near_copy(part, h).start()

    def near_sum():
        @pl.when(is_head)
        def _():
            cg_recv[c] = cg_stage[:, head_cols]
            for i in range(1, n_col):
                src = wrap(c + i, n_col)
                for part, (first, count) in enumerate(near_parts):
                    if count > 0:
                        block = cg_recv.at[src, pl.ds(first * rows, count * rows), :]
                        send(block, block, cg_ss.at[part, 0], cg_rs.at[part, src], on_col(src)).wait_recv()
            for i in range(2 * reach):
                at = pl.ds(i * rows, rows)
                total = cg_recv[0, at, :].astype(F32)
                for k in range(1, n_col):
                    total = total + cg_recv[k, at, :].astype(F32)
                cg_near[at, :] = total.astype(BF16)
            for i in range(2 * reach):
                @pl.when(is_own(i))
                def _(i=i):
                    cg_own[near_rows(i), :] = cg_near[held_at[i] * rows:(held_at[i] + 1) * rows, :]

                @pl.when(jnp.logical_not(is_own(i)))
                def _(i=i):
                    near_cross(i).start()

    def is_own(i):
        block = r + i - reach
        return jnp.logical_and(block >= 0, block < n_row)

    def near_block(i):
        return wrap(r + i - reach, n_row)

    def near_rows(i):
        return pl.ds(pl.multiple_of(near_block(i) * rows, rows), rows)

    def near_cross(i):
        return send(cg_near.at[pl.ds(held_at[i] * rows, rows), :], cg_own.at[near_rows(i), :],
                    cgx_ss.at[i], cgx_rs.at[near_block(i)], other)

    def cross_wait():
        for block in range(n_row):
            offset = block - r

            @pl.when(jnp.logical_or(offset < -reach, offset >= reach))
            def _(block=block):
                at = cg_own.at[pl.ds(block * rows, rows), :]
                send(at, at, cgx_ss.at[0], cgx_rs.at[block], other).wait_recv()

    def cg_drain():
        for part, (_, count) in enumerate(near_parts):
            if count > 0:
                for h in range(heads):
                    @pl.when(c != owner(h))
                    def _(part=part, h=h):
                        near_copy(part, h).wait_send()
        for i in range(2 * reach):
            @pl.when(jnp.logical_and(is_head, jnp.logical_not(is_own(i))))
            def _(i=i):
                near_cross(i).wait_send()

    drain.append(cg_drain)

    tile = cols // 3

    def project(first, last):
        tokens = ctx_rel[(middle - reach + first) * rows:(middle - reach + last) * rows, :]

        @pl.loop(0, 3)
        def _(i):
            at = pl.ds(pl.multiple_of(i * tile, tile), tile)
            product = jnp.dot(tokens, w_ref[:, at], preferred_element_type=F32)
            lo[first:last, :, at] = product.reshape(last - first, rows, tile)

    def project_ends():
        project(0, 2)
        if reach > 1:
            project(2 * reach - 2, 2 * reach)

    def project_middle():
        if reach > 2:
            project(2, 2 * reach - 2)

    def out_step(way, step, final=False):
        stage, landed = (rs_stage_r, rs_r) if way == 0 else (rs_stage_l, rs_l)
        place = (2 * reach - step) if way == 0 else step - 1
        for u in range(SUBS):
            total = lo[place, :, sub_cols[u]]
            if step > 1:
                block = landed.at[step - 2, :, sub_cols[u]]
                send(block, block, rs_ss.at[way, step - 2, u], rs_rs.at[way, step - 2, u], right).wait_recv()
                total = total + block[...].astype(F32)
            if final:
                lo[place, :, sub_cols[u]] = total
                continue
            stage[step - 1, :, sub_cols[u]] = total.astype(BF16)
            copy = send(stage.at[step - 1, :, sub_cols[u]], landed.at[step - 1, :, sub_cols[u]],
                        rs_ss.at[way, step - 1, u], rs_rs.at[way, step - 1, u], right if way == 0 else left)
            copy.start()
            (drain if step < 3 else late).append(copy.wait_send)

    def out_both(step):
        if step < reach:
            out_step(0, step)
        if step <= reach:
            out_step(1, step)

    stripe = cols // n_depth
    part = stripe // 2

    def weight_product(place, first, last):
        starts = (b * part_cols + place * LANES, b * part_cols + lines + lax.div(place, 2) * LANES)
        pair = [grad_all[first:last, :, pl.ds(pl.multiple_of(start, LANES), LANES)] for start in starts]
        tokens = jnp.concatenate(pair, axis=-1).reshape((last - first) * rows, 2 * LANES)
        return lax.dot_general(tokens, ctx_rel[first * rows:last * rows, :], TN, preferred_element_type=F32)

    def weight_near(first, last):
        @pl.loop(first, last)
        def _(place):
            dw_sum[place] = weight_product(place, middle - reach, middle + reach)

    def weight_far(place):
        place = wrap(place, n_y)
        dw_sum[place] += weight_product(place, 0, middle - reach) + weight_product(place, middle + reach, ring)

    def weight_step(way, step, final=False):
        place = wrap(wrap(y + (-step if way == 0 else step), n_y), n_y)
        if way == 0:
            total = dw_sum[place, 0:part, :]
        else:
            shared = pl.ds(pl.multiple_of(LANES + lax.rem(place, 2) * (LANES // 2), LANES // 2), LANES // 2)
            total = jnp.concatenate([dw_sum[place, part:LANES, :], dw_sum[place, shared, :]], axis=0)
        if step > 1:
            block = dw_recv.at[way, step - 2]
            send(block, block, dw_ss.at[way, step - 2], dw_rs.at[way, step - 2], up).wait_recv()
            total = total + block[...].astype(F32)
        if final:
            tile_start = b * (LANES // 2)
            if way == 0:
                dw_ref[pl.ds(pl.multiple_of(tile_start, LANES // 2), part), :] = total
            else:
                dw_ref[pl.ds(pl.multiple_of(tile_start + part, 32), LANES - part), :] = total[:LANES - part]
                dw_ref[pl.ds(pl.multiple_of((1 - b) * LANES, LANES), LANES // 2), :] = total[LANES - part:]
            return
        dw_stage[way, step - 1] = total.astype(BF16)
        copy = send(dw_stage.at[way, step - 1], dw_recv.at[way, step - 1], dw_ss.at[way, step - 1],
                    dw_rs.at[way, step - 1], up if way == 0 else down)
        copy.start()
        late.append(copy.wait_send)

    def backward():
        @pl.when(is_head)
        def _():
            cross_wait()
            for i in range(n_blocks):
                at = pl.ds(i * block_rows, block_rows)
                grad = cg_own[at, :]
                row_dot = jnp.sum(grad.astype(F32) * ctx_own[at, :].astype(F32), axis=-1, keepdims=True)
                dprob = lax.dot_general(grad, qkv[2], NT, preferred_element_type=F32)
                rounded = (probs[at, :] * (dprob - row_dot)).astype(BF16)
                dlogits[at, :] = rounded
                query_grad = jnp.dot(rounded, qkv[1], preferred_element_type=F32) * scale
                dqkv_own[0, at, :] = query_grad.astype(BF16)
            key_grad = lax.dot_general(dlogits[...], qkv[0], TN, preferred_element_type=F32) * scale
            dqkv_own[1] = key_grad.astype(BF16)
            value_grad = lax.dot_general(probs_b[...], cg_own[...], TN, preferred_element_type=F32)
            dqkv_own[2] = value_grad.astype(BF16)
            for i in range(1, n_col):
                dqkv_copy(i).start()
            for t in range(3):
                dqkv_all[t, :, head_cols] = dqkv_own[t, own_span, :]

    def dqkv_copy(i):
        to = wrap(c + i, n_col)
        return send(dqkv_own.at[:, pl.ds(pl.multiple_of(to * span, span), span), :],
                    dqkv_all.at[:, :, head_cols], dq_ss.at[i], dq_rs.at[head], on_col(to))

    def dqkv_drain():
        @pl.when(is_head)
        def _():
            for i in range(1, n_col):
                dqkv_copy(i).wait_send()

    late.append(dqkv_drain)

    def weight_ends():
        for way in range(2):
            if n_y > 2 or way == 0:
                weight_far(y + 2 * way - 1)
            weight_step(way, 1)

    def weight_rest():
        for offset in range(2, n_y - 1):
            weight_far(y + offset)
        weight_far(y)

    def weight_both(step):
        if step < n_y:
            weight_step(0, step)
            weight_step(1, step)

    def dqkv_finish():
        for h in range(heads):
            @pl.when(c != owner(h))
            def _(h=h):
                block = dqkv_all.at[:, :, fixed_cols[h]]
                send(block, block, dq_ss.at[0], dq_rs.at[h], right).wait_recv()
        for t, ref in enumerate((dq_ref, dk_ref, dv_ref)):
            ref[0] = dqkv_all[t]

    grad_step(1)
    heads_arrive()
    forward(0)
    cross_start(0)
    grad_step(2)
    forward(1)
    cross_relay(0)
    cross_start(1)
    ctx_start()
    cross_relay(1)
    cross_finish(0)
    grad_step(3)
    for copy in weight_copies:
        copy.wait()
    place_middles(w_mid, w_ref)
    context_grads(0)
    grad_step(4)
    context_grads(1)
    ctx_wait(0)
    grad_step(5)
    ctx_wait(1)
    ctx_in_order(middle - reach, middle + reach)
    project_ends()
    out_both(1)
    weight_near(0, n_y // 2)
    grad_step(6)
    project_middle()
    out_both(2)
    cross_finish(1)
    grad_step(7)
    near_sum()
    weight_near(n_y // 2, n_y)
    out_both(3)
    grad_step(8)
    ctx_wait(2)
    ctx_in_order(0, middle - reach)
    ctx_in_order(middle + reach, ring)
    weight_ends()
    weight_rest()
    out_both(4)
    weight_both(2)
    backward()
    weight_both(3)
    for wait in drain:
        wait()
    out_step(0, reach, final=True)
    out_step(1, reach + 1, final=True)
    for given, held in whole:
        out_ref[0, :, given] = lo[reach, :, held].astype(BF16)
    for n in range(0, n_y, 2):
        pair = swap_middles(lo[reach, :, middle_at(0, n)], lo[reach, :, middle_at(1, n)])
        for i in range(2):
            out_ref[0, :, middles[n + i]] = pair[i].astype(BF16)
    weight_step(0, n_y, final=True)
    weight_step(1, n_y, final=True)
    dqkv_finish()
    for wait in late:
        wait()


def hand_over(*refs):
    count = len(refs) // 3
    parts, outs, held = refs[:count], refs[count:2 * count], refs[2 * count:3 * count]
    sem = refs[-1]
    inward = [pltpu.make_async_copy(parts[i], held[i], sem.at[0, i]) for i in range(count)]
    outward = [pltpu.make_async_copy(held[i], outs[i], sem.at[1, i]) for i in range(count)]
    for copy in inward:
        copy.start()
    for i in range(count):
        inward[i].wait()
        outward[i].start()
    for copy in outward:
        copy.wait()


def solution(mesh):
    n_row, n_col, n_depth = mesh.shape["row"], mesh.shape["col"], mesh.shape["depth"]

    def local(q, k, v, positions, weight, grad):
        _, span, width = q.shape
        _, rows, cols = grad.shape
        length = positions.shape[1]
        heads, ring, reach, n_y = width // HEAD_DIM, HALVES * n_row, n_row // 2, n_depth // HALVES
        stripe = cols // n_depth
        vmem = pl.BlockSpec(memory_space=pltpu.VMEM)
        anywhere = pl.BlockSpec(memory_space=pltpu.HBM)
        dma = pltpu.SemaphoreType.DMA
        hops, turns = max(reach, 1), max(n_y - 1, 1)
        scratch = [
            pltpu.VMEM((width, cols), BF16),
            pltpu.VMEM((width, n_y * LANES), BF16),
            pltpu.VMEM((rows, n_y * LANES), BF16),
            pltpu.VMEM((3, span, width), BF16),
            pltpu.VMEM((3, length, HEAD_DIM), BF16),
            pltpu.VMEM((length, 128), F32),
            pltpu.VMEM((length, length), F32),
            pltpu.VMEM((length, length), BF16),
            pltpu.VMEM((length, length), BF16),
            pltpu.VMEM((length, HEAD_DIM), BF16),
            pltpu.VMEM((HALVES * length, width), BF16),
            pltpu.VMEM((HALVES * length, width), BF16),
            pltpu.VMEM((2, 2, length // 4, HEAD_DIM), BF16),
            pltpu.VMEM((ring, rows, cols), BF16),
            pltpu.VMEM((length, width), BF16),
            pltpu.VMEM((n_col, length, HEAD_DIM), BF16),
            pltpu.VMEM((length, HEAD_DIM), BF16),
            pltpu.VMEM((length, HEAD_DIM), BF16),
            pltpu.VMEM((3, length, HEAD_DIM), BF16),
            pltpu.VMEM((3, span, width), BF16),
            pltpu.VMEM((2 * reach, rows, cols), F32),
            pltpu.VMEM((hops, rows, cols), BF16),
            pltpu.VMEM((hops, rows, cols), BF16),
            pltpu.VMEM((hops, rows, cols), BF16),
            pltpu.VMEM((hops, rows, cols), BF16),
            pltpu.VMEM((n_y, 256, width), F32),
            pltpu.VMEM((2, turns, stripe // 2, width), BF16),
            pltpu.VMEM((2, turns, stripe // 2, width), BF16),
            dma((3 * n_y,)), dma((3 * n_y,)), dma((3,)),
            dma((heads,)), dma((n_col,)),
            dma((2, ring // 2, PARTS)), dma((2, ring // 2, PARTS)),
            dma((3, n_col)), dma((3, heads)), dma((2, 2, 2)), dma((2, 2, 2)),
            dma((2, heads)), dma((2, n_col)), dma((2 * reach,)), dma((n_row,)),
            dma((n_col,)), dma((heads,)),
            dma((2, hops, SUBS)), dma((2, hops, SUBS)),
            dma((2, turns)), dma((2, turns)),
        ]
        parts = pl.pallas_call(
            functools.partial(kernel, n_row, n_col, n_depth),
            out_shape=(
                jax.ShapeDtypeStruct(grad.shape, BF16),
                jax.ShapeDtypeStruct(q.shape, BF16),
                jax.ShapeDtypeStruct(k.shape, BF16),
                jax.ShapeDtypeStruct(v.shape, BF16),
                jax.ShapeDtypeStruct((stripe, width), F32),
            ),
            in_specs=[anywhere] * 3 + [vmem] + [anywhere] * 2,
            out_specs=(vmem,) * 5,
            scratch_shapes=scratch,
            compiler_params=pltpu.CompilerParams(
                collective_id=0, has_side_effects=True, vmem_limit_bytes=VMEM_BYTES
            ),
        )(q, k, v, positions, weight, grad)
        *parts, weight_grad = pl.pallas_call(
            hand_over,
            out_shape=[jax.ShapeDtypeStruct(part.shape, part.dtype) for part in parts],
            in_specs=[anywhere] * len(parts),
            out_specs=[anywhere] * len(parts),
            scratch_shapes=[pltpu.VMEM(part.shape, part.dtype) for part in parts] + [dma((2, len(parts)))],
            compiler_params=pltpu.CompilerParams(vmem_limit_bytes=VMEM_BYTES),
        )(*parts)
        return *parts, weight_grad.T

    return jax.shard_map(
        local,
        mesh=mesh,
        in_specs=(
            P("depth", "col", "row"),
            P("depth", "col", "row"),
            P("depth", "col", "row"),
            P("depth", None),
            P("row", "col"),
            P("depth", "row", "col"),
        ),
        out_specs=(
            P("depth", "row", "col"),
            P("depth", "col", "row"),
            P("depth", "col", "row"),
            P("depth", "col", "row"),
            P("row", ("col", "depth")),
        ),
        check_vma=False,
    )
```

```python
import functools

import jax
import jax.numpy as jnp
from jax import lax
from jax.experimental import pallas as pl
from jax.experimental.pallas import tpu as pltpu
from jax.sharding import PartitionSpec as P

HEAD_DIM = 128
HALVES = 2
PARTS = 2
SUBS = 2
LANES = 128
VMEM_BYTES = 56 * 1024 * 1024
MESH = pl.DeviceIdType.MESH
F32, BF16 = jnp.float32, jnp.bfloat16

NT = (((1,), (1,)), ((), ()))
TN = (((0,), (0,)), ((), ()))


def kernel(
    n_row, n_col, n_depth,
    q_ref, k_ref, v_ref, pos_ref, w_hbm, g_ref,
    out_ref, dq_ref, dk_ref, dv_ref, dw_ref,
    w_ref, w_mid, g_mid, qkv_stage, qkv, pos_col, probs, probs_b, dlogits, ctx_own, ctx_all, ctx_rel, relay, grad_all,
    cg_stage, cg_recv, cg_near, cg_own, dqkv_own, dqkv_all,
    lo, rs_stage_r, rs_stage_l, rs_r, rs_l, dw_sum, dw_stage, dw_recv,
    w_sem, g_sem, in_sem, qkv_ss, qkv_rs, ag_ss, ag_rs, ctx_ss, ctx_rs, cross_ss, cross_rs, cg_ss, cg_rs, cgx_ss, cgx_rs, dq_ss, dq_rs,
    rs_ss, rs_rs, dw_ss, dw_rs,
):
    r, c, d = lax.axis_index("row"), lax.axis_index("col"), lax.axis_index("depth")
    y, b = lax.div(d, HALVES), lax.rem(d, HALVES)
    ring, n_y = HALVES * n_row, n_depth // HALVES
    reach = n_row // 2
    z = b * n_row + r
    span, width = q_ref.shape[1:]
    rows, cols = g_ref.shape[1:]
    length = pos_ref.shape[1]
    heads = width // HEAD_DIM
    scale = HEAD_DIM ** (-0.5)

    def wrap(place, size):
        place = jnp.where(place < 0, place + size, place)
        return jnp.where(place >= size, place - size, place)

    def in_half(place):
        half = jnp.where(place >= n_row, 1, 0)
        return place - half * n_row, half

    def on_ring(place):
        line, half = in_half(wrap(place, ring))
        return (line, c, y * HALVES + half)

    def on_col(place):
        return (r, place, d)

    def on_y(place):
        return (r, c, wrap(place, n_y) * HALVES + b)

    def chunk_at(offset):
        return wrap(z + offset, ring)

    def owner(h):
        return (h * n_col) // heads

    right, left, up, down = on_ring(z + 1), on_ring(z - 1), on_y(y + 1), on_y(y - 1)
    far_right, far_left, other = on_ring(z + n_row - 1), on_ring(z - n_row + 1), on_ring(z + n_row)
    middle = ring // 2
    head, is_head = 0, c == owner(0)
    for h in range(1, heads):
        head = jnp.where(c >= owner(h), h, head)
        is_head = jnp.logical_or(is_head, c == owner(h))
    head_cols = pl.ds(pl.multiple_of(head * HEAD_DIM, HEAD_DIM), HEAD_DIM)
    fixed_cols = [pl.ds(h * HEAD_DIM, HEAD_DIM) for h in range(heads)]
    sub_cols = [pl.ds(u * (cols // SUBS), cols // SUBS) for u in range(SUBS)]

    def send(src, dst, send_sem, recv_sem, to):
        return pltpu.make_async_remote_copy(
            src_ref=src, dst_ref=dst, send_sem=send_sem, recv_sem=recv_sem,
            device_id=to, device_id_type=MESH,
        )

    barrier = pltpu.get_barrier_semaphore()
    peers = [on_col(wrap(c + i, n_col)) for i in range(1, n_col)]
    peers += [right, left, other, up]
    if n_y > 2:
        peers += [down]
    if n_row > 2:
        peers += [far_right, far_left]
    for peer in peers:
        pl.semaphore_signal(barrier, inc=1, device_id=peer, device_id_type=MESH)
    part_cols = cols // PARTS
    lines = n_y * LANES
    whole = [(pl.ds((n * 3 + 2 * u) * LANES, LANES), pl.ds(u * part_cols + n * LANES, LANES))
             for n in range(n_y) for u in range(PARTS)]
    middles = [pl.ds((n * 3 + 1) * LANES, LANES) for n in range(n_y)]

    def middle_at(u, n):
        return pl.ds(u * part_cols + lines + (n // 2) * LANES, LANES)

    def swap_middles(first, second):
        lower = lax.broadcasted_iota(jnp.int32, first.shape, 1) < LANES // 2
        return (jnp.where(lower, first, pltpu.roll(second, LANES // 2, 1)),
                jnp.where(lower, pltpu.roll(first, LANES // 2, 1), second))

    def place_middles(staged, held):
        for n in range(0, n_y, 2):
            pair = [staged[:, (n + i) * LANES:(n + i + 1) * LANES].astype(F32) for i in range(2)]
            for u, tile_values in enumerate(swap_middles(*pair)):
                held[:, middle_at(u, n)] = tile_values.astype(BF16)

    weight_copies = [pltpu.make_async_copy(w_hbm.at[:, given], w_ref.at[:, held], w_sem.at[i])
                     for i, (given, held) in enumerate(whole)]
    weight_copies += [pltpu.make_async_copy(w_hbm.at[:, given], w_mid.at[:, pl.ds(n * LANES, LANES)], w_sem.at[2 * n_y + n])
                      for n, given in enumerate(middles)]
    head_copies = [pltpu.make_async_copy(ref.at[0], qkv_stage.at[t], in_sem.at[t])
                   for t, ref in enumerate((q_ref, k_ref, v_ref))]
    grad_copies = [pltpu.make_async_copy(g_ref.at[0, :, given], grad_all.at[middle, :, held], g_sem.at[i])
                   for i, (given, held) in enumerate(whole)]
    grad_copies += [pltpu.make_async_copy(g_ref.at[0, :, given], g_mid.at[:, pl.ds(n * LANES, LANES)], g_sem.at[2 * n_y + n])
                    for n, given in enumerate(middles)]
    for copy in grad_copies + head_copies + weight_copies:
        copy.start()
    for copy in grad_copies:
        copy.wait()
    place_middles(g_mid, grad_all.at[middle])
    pl.semaphore_wait(barrier, len(peers))

    drain, late = [], []

    far = [ring // 2, ring // 2 - 1]
    near = [reach, reach - 1]
    held_cols = [pl.ds(u * part_cols, part_cols) for u in range(PARTS)]

    def grad_copy(way, step, u):
        sign = -1 if way == 0 else 1
        return send(grad_all.at[middle + sign * (step - 1), :, held_cols[u]],
                    grad_all.at[middle + sign * step, :, held_cols[u]],
                    ag_ss.at[way, step - 1, u], ag_rs.at[way, step - 1, u], right if way == 0 else left)

    def where_needed(place, way, step, u, action):
        if step <= near[way]:
            action()
            return
        line, half = in_half(wrap(place, ring))
        onward = far[way] - step
        crosses = line + onward >= n_row if way == 0 else line - onward < 0
        pl.when(jnp.logical_or(crosses, half == u))(action)

    def grad_start(way, step, u):
        where_needed(z + (1 if way == 0 else -1), way, step, u, grad_copy(way, step, u).start)

    def grad_step(step):
        for u in range(PARTS):
            for way in range(2):
                if step <= far[way]:
                    def pass_on(way=way, u=u):
                        grad_copy(way, step, u).wait_recv()
                        if step < far[way]:
                            grad_start(way, step + 1, u)

                    where_needed(z, way, step, u, pass_on)

    def grad_drain():
        for way in range(2):
            for step in range(1, far[way] + 1):
                for u in range(PARTS):
                    where_needed(z + (1 if way == 0 else -1), way, step, u, grad_copy(way, step, u).wait_send)

    drain.append(grad_drain)
    for u in range(PARTS):
        for way in range(2):
            grad_start(way, 1, u)

    own_span = pl.ds(pl.multiple_of(c * span, span), span)
    for copy in head_copies:
        copy.wait()
    def heads_copy(h):
        return send(qkv_stage.at[:, :, fixed_cols[h]], qkv.at[:, own_span, :],
                    qkv_ss.at[h], qkv_rs.at[c], on_col(owner(h)))

    for h in range(heads):
        @pl.when(c != owner(h))
        def _(h=h):
            heads_copy(h).start()

    @pl.when(is_head)
    def _():
        for t in range(3):
            qkv[t, own_span, :] = qkv_stage[t, :, head_cols]

    def heads_drain():
        for h in range(heads):
            @pl.when(c != owner(h))
            def _(h=h):
                heads_copy(h).wait_send()

    drain.append(heads_drain)

    block_rows = min(128, length)

    def forward(phase):
        @pl.when(is_head)
        def _():
            base = crossing_half(r, phase) * half_rows
            for i in range(n_blocks // 2):
                at = pl.ds(pl.multiple_of(base + i * block_rows, block_rows), block_rows)
                logits = lax.dot_general(qkv[0, at, :], qkv[1], NT, preferred_element_type=F32)
                visible = pos_ref[...].astype(F32) <= pos_col[at, 0:1]
                logits = jnp.where(visible, logits * scale, -jnp.inf)
                highest = jnp.max(logits, axis=-1, keepdims=True)
                grown = jnp.exp(logits - highest)
                prob = grown * (1.0 / jnp.sum(grown, axis=-1, keepdims=True))
                probs[at, :] = prob
                rounded = prob.astype(BF16)
                probs_b[at, :] = rounded
                context = jnp.dot(rounded, qkv[2], preferred_element_type=F32)
                ctx_own[at, :] = context.astype(BF16)

    n_blocks = length // block_rows

    def heads_arrive():
        @pl.when(is_head)
        def _():
            pos_col[...] = jnp.transpose(
                jnp.broadcast_to(pos_ref[...].astype(F32), (128, length))
            )
            for i in range(1, n_col):
                src = wrap(c + i, n_col)
                place = qkv.at[:, pl.ds(pl.multiple_of(src * span, span), span), :]
                send(place, place, qkv_ss.at[0], qkv_rs.at[src], on_col(src)).wait_recv()

    half_rows, quarter = length // 2, length // 4

    def ctx_rows(group):
        if group == 0:
            return pl.ds(pl.multiple_of(b * length, length), length)
        return crossing_rows(1 - b, r, group - 1)

    def crossing_half(line, phase):
        return jnp.where(line < reach, 1 - phase, phase)

    def crossing_rows(place, line, phase):
        start = place * length + crossing_half(line, phase) * half_rows
        return pl.ds(pl.multiple_of(start, half_rows), half_rows)

    def crossing_part(place, line, phase, way):
        start = place * length + crossing_half(line, phase) * half_rows + way * quarter
        return pl.ds(pl.multiple_of(start, quarter), quarter)

    def cross_copy(phase, way):
        return send(ctx_own.at[crossing_part(0, r, phase, way), :], relay.at[phase, way],
                    cross_ss.at[0, phase, way], cross_rs.at[0, phase, way], right if way == 0 else left)

    def relay_copy(phase, way):
        origin = chunk_at(-1 if way == 0 else 1)
        line, half = in_half(origin)
        at = crossing_part(half, line, phase, way)
        return send(relay.at[phase, way], ctx_all.at[at, head_cols],
                    cross_ss.at[1, phase, way], cross_rs.at[1, phase, way], far_right if way == 0 else far_left)

    def cross_arrives(phase, way):
        block = ctx_all.at[crossing_part(1 - b, r, phase, way), head_cols]
        send(block, block, cross_ss.at[1, phase, way], cross_rs.at[1, phase, way], far_right).wait_recv()

    def ctx_copies(group):
        src = ctx_own if group == 0 else ctx_all.at[ctx_rows(group), head_cols]
        targets = [on_col(wrap(c + i, n_col)) for i in range(1, n_col)]
        return [
            send(src, ctx_all.at[ctx_rows(group), head_cols], ctx_ss.at[group, i], ctx_rs.at[group, head], to)
            for i, to in enumerate(targets)
        ]

    def ctx_block(half, h):
        block = ctx_all.at[ctx_rows(half), fixed_cols[h]]
        return send(block, block, ctx_ss.at[0, 0], ctx_rs.at[half, h], right)

    def ctx_wait(half):
        for h in range(heads):
            @pl.when(c != owner(h))
            def _(h=h):
                ctx_block(half, h).wait_recv()

    def cross_start(phase):
        @pl.when(is_head)
        def _():
            for way in range(2):
                cross_copy(phase, way).start()

    def ctx_start():
        @pl.when(is_head)
        def _():
            for copy in ctx_copies(0):
                copy.start()
            ctx_all[ctx_rows(0), head_cols] = ctx_own[...]

    def cross_relay(phase):
        @pl.when(is_head)
        def _():
            for way in range(2):
                cross_copy(phase, way).wait_recv()
                relay_copy(phase, way).start()

    def cross_finish(phase):
        @pl.when(is_head)
        def _():
            for way in range(2):
                cross_arrives(phase, way)
            for copy in ctx_copies(1 + phase):
                copy.start()

    def ctx_in_order(first, last):
        for slot in range(first, last):
            held = chunk_at(slot - middle)
            ctx_rel[slot * rows:(slot + 1) * rows, :] = ctx_all[pl.ds(pl.multiple_of(held * rows, rows), rows), :]

    def ctx_drain():
        @pl.when(is_head)
        def _():
            for phase in range(2):
                for way in range(2):
                    cross_copy(phase, way).wait_send()
                    relay_copy(phase, way).wait_send()
            for group in range(3):
                for copy in ctx_copies(group):
                    copy.wait_send()
    drain.append(ctx_drain)

    inner = reach // 2
    near_slots = [list(range(reach - inner, reach + inner)),
                  list(range(reach - inner)) + list(range(reach + inner, 2 * reach))]
    held_at = {slot: i for i, slot in enumerate(near_slots[0] + near_slots[1])}
    near_parts = [(0, 2 * inner), (2 * inner, 2 * reach - 2 * inner)]

    def near_copy(part, h):
        at = pl.ds(near_parts[part][0] * rows, near_parts[part][1] * rows)
        return send(cg_stage.at[at, fixed_cols[h]], cg_recv.at[c, at, :],
                    cg_ss.at[part, h], cg_rs.at[part, c], on_col(owner(h)))

    def context_grads(part):
        first, count = near_parts[part]
        if count == 0:
            return
        tokens = jnp.concatenate([grad_all[middle - reach + slot] for slot in near_slots[part]], axis=0)
        for i in range(heads // 2):
            two = pl.ds(i * 2 * HEAD_DIM, 2 * HEAD_DIM)
            product = lax.dot_general(tokens, w_ref[two, :], NT, preferred_element_type=F32)
            cg_stage[first * rows:(first + count) * rows, two] = product.astype(BF16)
            for h in (2 * i, 2 * i + 1):
                @pl.when(c != owner(h))
                def _(h=h):
                    near_copy(part, h).start()

    def near_sum():
        @pl.when(is_head)
        def _():
            cg_recv[c] = cg_stage[:, head_cols]
            for i in range(1, n_col):
                src = wrap(c + i, n_col)
                for part, (first, count) in enumerate(near_parts):
                    if count > 0:
                        block = cg_recv.at[src, pl.ds(first * rows, count * rows), :]
                        send(block, block, cg_ss.at[part, 0], cg_rs.at[part, src], on_col(src)).wait_recv()
            for i in range(2 * reach):
                at = pl.ds(i * rows, rows)
                total = cg_recv[0, at, :].astype(F32)
                for k in range(1, n_col):
                    total = total + cg_recv[k, at, :].astype(F32)
                cg_near[at, :] = total.astype(BF16)
            for i in range(2 * reach):
                @pl.when(is_own(i))
                def _(i=i):
                    cg_own[near_rows(i), :] = cg_near[held_at[i] * rows:(held_at[i] + 1) * rows, :]

                @pl.when(jnp.logical_not(is_own(i)))
                def _(i=i):
                    near_cross(i).start()

    def is_own(i):
        block = r + i - reach
        return jnp.logical_and(block >= 0, block < n_row)

    def near_block(i):
        return wrap(r + i - reach, n_row)

    def near_rows(i):
        return pl.ds(pl.multiple_of(near_block(i) * rows, rows), rows)

    def near_cross(i):
        return send(cg_near.at[pl.ds(held_at[i] * rows, rows), :], cg_own.at[near_rows(i), :],
                    cgx_ss.at[i], cgx_rs.at[near_block(i)], other)

    def cross_wait():
        for block in range(n_row):
            offset = block - r

            @pl.when(jnp.logical_or(offset < -reach, offset >= reach))
            def _(block=block):
                at = cg_own.at[pl.ds(block * rows, rows), :]
                send(at, at, cgx_ss.at[0], cgx_rs.at[block], other).wait_recv()

    def cg_drain():
        for part, (_, count) in enumerate(near_parts):
            if count > 0:
                for h in range(heads):
                    @pl.when(c != owner(h))
                    def _(part=part, h=h):
                        near_copy(part, h).wait_send()
        for i in range(2 * reach):
            @pl.when(jnp.logical_and(is_head, jnp.logical_not(is_own(i))))
            def _(i=i):
                near_cross(i).wait_send()

    drain.append(cg_drain)

    tile = cols // 3

    def project(first, last):
        tokens = ctx_rel[(middle - reach + first) * rows:(middle - reach + last) * rows, :]

        @pl.loop(0, 3)
        def _(i):
            at = pl.ds(pl.multiple_of(i * tile, tile), tile)
            product = jnp.dot(tokens, w_ref[:, at], preferred_element_type=F32)
            lo[first:last, :, at] = product.reshape(last - first, rows, tile)

    def project_ends():
        project(0, 2)
        if reach > 1:
            project(2 * reach - 2, 2 * reach)

    def project_middle():
        if reach > 2:
            project(2, 2 * reach - 2)

    def out_step(way, step, final=False):
        stage, landed = (rs_stage_r, rs_r) if way == 0 else (rs_stage_l, rs_l)
        place = (2 * reach - step) if way == 0 else step - 1
        for u in range(SUBS):
            total = lo[place, :, sub_cols[u]]
            if step > 1:
                block = landed.at[step - 2, :, sub_cols[u]]
                send(block, block, rs_ss.at[way, step - 2, u], rs_rs.at[way, step - 2, u], right).wait_recv()
                total = total + block[...].astype(F32)
            if final:
                lo[place, :, sub_cols[u]] = total
                continue
            stage[step - 1, :, sub_cols[u]] = total.astype(BF16)
            copy = send(stage.at[step - 1, :, sub_cols[u]], landed.at[step - 1, :, sub_cols[u]],
                        rs_ss.at[way, step - 1, u], rs_rs.at[way, step - 1, u], right if way == 0 else left)
            copy.start()
            (drain if step < 3 else late).append(copy.wait_send)

    def out_both(step):
        if step < reach:
            out_step(0, step)
        if step <= reach:
            out_step(1, step)

    stripe = cols // n_depth
    part = stripe // 2

    def weight_product(place, first, last):
        starts = (b * part_cols + place * LANES, b * part_cols + lines + lax.div(place, 2) * LANES)
        pair = [grad_all[first:last, :, pl.ds(pl.multiple_of(start, LANES), LANES)] for start in starts]
        tokens = jnp.concatenate(pair, axis=-1).reshape((last - first) * rows, 2 * LANES)
        return lax.dot_general(tokens, ctx_rel[first * rows:last * rows, :], TN, preferred_element_type=F32)

    def weight_near(first, last):
        @pl.loop(first, last)
        def _(place):
            dw_sum[place] = weight_product(place, middle - reach, middle + reach)

    def weight_far(place):
        place = wrap(place, n_y)
        dw_sum[place] += weight_product(place, 0, middle - reach) + weight_product(place, middle + reach, ring)

    def weight_step(way, step, final=False):
        place = wrap(wrap(y + (-step if way == 0 else step), n_y), n_y)
        if way == 0:
            total = dw_sum[place, 0:part, :]
        else:
            shared = pl.ds(pl.multiple_of(LANES + lax.rem(place, 2) * (LANES // 2), LANES // 2), LANES // 2)
            total = jnp.concatenate([dw_sum[place, part:LANES, :], dw_sum[place, shared, :]], axis=0)
        if step > 1:
            block = dw_recv.at[way, step - 2]
            send(block, block, dw_ss.at[way, step - 2], dw_rs.at[way, step - 2], up).wait_recv()
            total = total + block[...].astype(F32)
        if final:
            tile_start = b * (LANES // 2)
            if way == 0:
                dw_ref[pl.ds(pl.multiple_of(tile_start, LANES // 2), part), :] = total
            else:
                dw_ref[pl.ds(pl.multiple_of(tile_start + part, 32), LANES - part), :] = total[:LANES - part]
                dw_ref[pl.ds(pl.multiple_of((1 - b) * LANES, LANES), LANES // 2), :] = total[LANES - part:]
            return
        dw_stage[way, step - 1] = total.astype(BF16)
        copy = send(dw_stage.at[way, step - 1], dw_recv.at[way, step - 1], dw_ss.at[way, step - 1],
                    dw_rs.at[way, step - 1], up if way == 0 else down)
        copy.start()
        late.append(copy.wait_send)

    def backward():
        @pl.when(is_head)
        def _():
            cross_wait()
            for i in range(n_blocks):
                at = pl.ds(i * block_rows, block_rows)
                grad = cg_own[at, :]
                row_dot = jnp.sum(grad.astype(F32) * ctx_own[at, :].astype(F32), axis=-1, keepdims=True)
                dprob = lax.dot_general(grad, qkv[2], NT, preferred_element_type=F32)
                rounded = (probs[at, :] * (dprob - row_dot)).astype(BF16)
                dlogits[at, :] = rounded
                query_grad = jnp.dot(rounded, qkv[1], preferred_element_type=F32) * scale
                dqkv_own[0, at, :] = query_grad.astype(BF16)
            key_grad = lax.dot_general(dlogits[...], qkv[0], TN, preferred_element_type=F32) * scale
            dqkv_own[1] = key_grad.astype(BF16)
            value_grad = lax.dot_general(probs_b[...], cg_own[...], TN, preferred_element_type=F32)
            dqkv_own[2] = value_grad.astype(BF16)
            for i in range(1, n_col):
                dqkv_copy(i).start()
            for t in range(3):
                dqkv_all[t, :, head_cols] = dqkv_own[t, own_span, :]

    def dqkv_copy(i):
        to = wrap(c + i, n_col)
        return send(dqkv_own.at[:, pl.ds(pl.multiple_of(to * span, span), span), :],
                    dqkv_all.at[:, :, head_cols], dq_ss.at[i], dq_rs.at[head], on_col(to))

    def dqkv_drain():
        @pl.when(is_head)
        def _():
            for i in range(1, n_col):
                dqkv_copy(i).wait_send()

    late.append(dqkv_drain)

    def weight_ends():
        for way in range(2):
            if n_y > 2 or way == 0:
                weight_far(y + 2 * way - 1)
            weight_step(way, 1)

    def weight_rest():
        for offset in range(2, n_y - 1):
            weight_far(y + offset)
        weight_far(y)

    def weight_both(step):
        if step < n_y:
            weight_step(0, step)
            weight_step(1, step)

    def dqkv_finish():
        for h in range(heads):
            @pl.when(c != owner(h))
            def _(h=h):
                block = dqkv_all.at[:, :, fixed_cols[h]]
                send(block, block, dq_ss.at[0], dq_rs.at[h], right).wait_recv()
        for t, ref in enumerate((dq_ref, dk_ref, dv_ref)):
            ref[0] = dqkv_all[t]

    grad_step(1)
    heads_arrive()
    forward(0)
    cross_start(0)
    grad_step(2)
    forward(1)
    cross_relay(0)
    cross_start(1)
    ctx_start()
    cross_relay(1)
    cross_finish(0)
    grad_step(3)
    for copy in weight_copies:
        copy.wait()
    place_middles(w_mid, w_ref)
    context_grads(0)
    grad_step(4)
    context_grads(1)
    ctx_wait(0)
    grad_step(5)
    ctx_wait(1)
    ctx_in_order(middle - reach, middle + reach)
    project_ends()
    out_both(1)
    grad_step(6)
    project_middle()
    out_both(2)
    cross_finish(1)
    grad_step(7)
    near_sum()
    weight_near(0, n_y)
    out_both(3)
    ctx_wait(2)
    grad_step(8)
    ctx_in_order(0, middle - reach)
    ctx_in_order(middle + reach, ring)
    weight_ends()
    weight_rest()
    out_both(4)
    weight_both(2)
    backward()
    weight_both(3)
    for wait in drain:
        wait()
    out_step(0, reach, final=True)
    out_step(1, reach + 1, final=True)
    for given, held in whole:
        out_ref[0, :, given] = lo[reach, :, held].astype(BF16)
    for n in range(0, n_y, 2):
        pair = swap_middles(lo[reach, :, middle_at(0, n)], lo[reach, :, middle_at(1, n)])
        for i in range(2):
            out_ref[0, :, middles[n + i]] = pair[i].astype(BF16)
    weight_step(0, n_y, final=True)
    weight_step(1, n_y, final=True)
    dqkv_finish()
    for wait in late:
        wait()


def hand_over(*refs):
    count = len(refs) // 3
    parts, outs, held = refs[:count], refs[count:2 * count], refs[2 * count:3 * count]
    sem = refs[-1]
    inward = [pltpu.make_async_copy(parts[i], held[i], sem.at[0, i]) for i in range(count)]
    outward = [pltpu.make_async_copy(held[i], outs[i], sem.at[1, i]) for i in range(count)]
    for copy in inward:
        copy.start()
    for i in range(count):
        inward[i].wait()
        outward[i].start()
    for copy in outward:
        copy.wait()


def solution(mesh):
    n_row, n_col, n_depth = mesh.shape["row"], mesh.shape["col"], mesh.shape["depth"]

    def local(q, k, v, positions, weight, grad):
        _, span, width = q.shape
        _, rows, cols = grad.shape
        length = positions.shape[1]
        heads, ring, reach, n_y = width // HEAD_DIM, HALVES * n_row, n_row // 2, n_depth // HALVES
        stripe = cols // n_depth
        vmem = pl.BlockSpec(memory_space=pltpu.VMEM)
        anywhere = pl.BlockSpec(memory_space=pltpu.HBM)
        dma = pltpu.SemaphoreType.DMA
        hops, turns = max(reach, 1), max(n_y - 1, 1)
        scratch = [
            pltpu.VMEM((width, cols), BF16),
            pltpu.VMEM((width, n_y * LANES), BF16),
            pltpu.VMEM((rows, n_y * LANES), BF16),
            pltpu.VMEM((3, span, width), BF16),
            pltpu.VMEM((3, length, HEAD_DIM), BF16),
            pltpu.VMEM((length, 128), F32),
            pltpu.VMEM((length, length), F32),
            pltpu.VMEM((length, length), BF16),
            pltpu.VMEM((length, length), BF16),
            pltpu.VMEM((length, HEAD_DIM), BF16),
            pltpu.VMEM((HALVES * length, width), BF16),
            pltpu.VMEM((HALVES * length, width), BF16),
            pltpu.VMEM((2, 2, length // 4, HEAD_DIM), BF16),
            pltpu.VMEM((ring, rows, cols), BF16),
            pltpu.VMEM((length, width), BF16),
            pltpu.VMEM((n_col, length, HEAD_DIM), BF16),
            pltpu.VMEM((length, HEAD_DIM), BF16),
            pltpu.VMEM((length, HEAD_DIM), BF16),
            pltpu.VMEM((3, length, HEAD_DIM), BF16),
            pltpu.VMEM((3, span, width), BF16),
            pltpu.VMEM((2 * reach, rows, cols), F32),
            pltpu.VMEM((hops, rows, cols), BF16),
            pltpu.VMEM((hops, rows, cols), BF16),
            pltpu.VMEM((hops, rows, cols), BF16),
            pltpu.VMEM((hops, rows, cols), BF16),
            pltpu.VMEM((n_y, 256, width), F32),
            pltpu.VMEM((2, turns, stripe // 2, width), BF16),
            pltpu.VMEM((2, turns, stripe // 2, width), BF16),
            dma((3 * n_y,)), dma((3 * n_y,)), dma((3,)),
            dma((heads,)), dma((n_col,)),
            dma((2, ring // 2, PARTS)), dma((2, ring // 2, PARTS)),
            dma((3, n_col)), dma((3, heads)), dma((2, 2, 2)), dma((2, 2, 2)),
            dma((2, heads)), dma((2, n_col)), dma((2 * reach,)), dma((n_row,)),
            dma((n_col,)), dma((heads,)),
            dma((2, hops, SUBS)), dma((2, hops, SUBS)),
            dma((2, turns)), dma((2, turns)),
        ]
        parts = pl.pallas_call(
            functools.partial(kernel, n_row, n_col, n_depth),
            out_shape=(
                jax.ShapeDtypeStruct(grad.shape, BF16),
                jax.ShapeDtypeStruct(q.shape, BF16),
                jax.ShapeDtypeStruct(k.shape, BF16),
                jax.ShapeDtypeStruct(v.shape, BF16),
                jax.ShapeDtypeStruct((stripe, width), F32),
            ),
            in_specs=[anywhere] * 3 + [vmem] + [anywhere] * 2,
            out_specs=(vmem,) * 5,
            scratch_shapes=scratch,
            compiler_params=pltpu.CompilerParams(
                collective_id=0, has_side_effects=True, vmem_limit_bytes=VMEM_BYTES
            ),
        )(q, k, v, positions, weight, grad)
        *parts, weight_grad = pl.pallas_call(
            hand_over,
            out_shape=[jax.ShapeDtypeStruct(part.shape, part.dtype) for part in parts],
            in_specs=[anywhere] * len(parts),
            out_specs=[anywhere] * len(parts),
            scratch_shapes=[pltpu.VMEM(part.shape, part.dtype) for part in parts] + [dma((2, len(parts)))],
            compiler_params=pltpu.CompilerParams(vmem_limit_bytes=VMEM_BYTES),
        )(*parts)
        return *parts, weight_grad.T

    return jax.shard_map(
        local,
        mesh=mesh,
        in_specs=(
            P("depth", "col", "row"),
            P("depth", "col", "row"),
            P("depth", "col", "row"),
            P("depth", None),
            P("row", "col"),
            P("depth", "row", "col"),
        ),
        out_specs=(
            P("depth", "row", "col"),
            P("depth", "col", "row"),
            P("depth", "col", "row"),
            P("depth", "col", "row"),
            P("row", ("col", "depth")),
        ),
        check_vma=False,
    )
```
